32 devices in a mesh: grp: 4 (over z), dev: 8 (over y, x, core).
Axes of the slice: x: 2, y: 2, z: 4, core: 2. Of those that a mesh axis runs over, the one named last changes fastest.
Arguments:
- velocity_old: float32 [128, 3, 32, 1024], P(('grp', 'dev')), may hold values from -6 to 6
- viscosity_old: float32 [128, 32, 1024], P(('grp', 'dev')), may hold values from 0.25 to 4
- source: int32 [128], replicated, may hold values from 0 to 127, as said below
Outputs:
- velocity_new: float32 [128, 3, 32, 1024], P(('grp', 'dev'))
The draws below stay inside these ranges and needn't reach their ends.
Inputs may be any that keep to these rules, and one draw needn't show every extreme that they name: `source`: A permutation; the old block of new block b lies in the same agglomeration group and has the same place among its device's 4 blocks; the 4 blocks of a new device come from 4 different old devices of its group, and each old device sends 1 block to each of 4 different new devices.
All inputs are finite; a program needn't handle non-finite values.
Results may differ from the reference program's by a relative error of at most 0.0001.
Values sent between devices are 32-bit elements; how exact they have to be, the bound alone decides.
No kernel may reach another device: no remote copies, remote signals or barrier semaphores. Data moves between devices by JAX's collectives and lax.ppermute only.
A program may use at most 256 MiB of HBM per device.

```python
import math
import jax
import jax.numpy as jnp

SIDE = 32
BLK_DEV = 4
SWEEPS = 2
BOTTOM = 8
BLOCKS = 128
N_GRP = 4
N_DEV = 8


def draw_source(key, part):

    def one_group(group_no):
        group_key = jax.random.fold_in(key, group_no)
        order = jax.random.permutation(jax.random.fold_in(group_key, 1), N_DEV)
        steps = jax.random.permutation(jax.random.fold_in(group_key, 2), N_DEV - 1)[:BLK_DEV - 1] + 1
        offsets = jnp.concatenate([jnp.zeros((1,), jnp.int32), steps.astype(jnp.int32)])
        member_ids = jnp.arange(N_DEV, dtype=jnp.int32)
        owners = order[(member_ids[:, None] + offsets[None, :]) % N_DEV]
        return ((group_no * N_DEV + owners) * BLK_DEV + jnp.arange(BLK_DEV, dtype=jnp.int32)[None, :]).astype(jnp.int32)
    return jax.vmap(one_group)(jnp.arange(N_GRP, dtype=jnp.int32)).reshape(BLOCKS).astype(jnp.int32)


def block_scale(stream_key, shape, shards, low, largest):
    level, own = 1.0, jax.random.fold_in(stream_key, 6)
    for axis_at, shards_of in shards:
        steps = jnp.exp(jax.random.uniform(jax.random.fold_in(own, axis_at), (shards_of,), jnp.float32, low / len(shards), largest / len(shards)))
        level = level * jnp.repeat(steps, shape[axis_at] // shards_of).reshape([-1 if axis == axis_at else 1 for axis in range(len(shape))])
    return level


def bell_draw(own_key, shape, width, bound, shards=(), held_as=jnp.bfloat16):
    level = block_scale(own_key, shape, shards, -0.22, 0.18) if shards else 1.0
    values = jax.random.normal(own_key, shape, jnp.float32) * width * level
    return jnp.minimum(jnp.maximum(values, -bound), bound).astype(held_as)


def setup_inputs(seed: int = 0) -> dict:
    splits = jax.random.split(jax.random.key(seed), 4)
    return {
        "velocity_old": bell_draw(splits[0], (BLOCKS, 3, SIDE, SIDE * SIDE), 1.0, 6.0, ((0, 32),), jnp.float32),
        "viscosity_old": jnp.clip(jnp.exp(math.log(4.0) - 2.7725887 * jax.random.uniform(splits[1], (BLOCKS, SIDE, SIDE * SIDE), jnp.float32) ** block_scale(splits[1], (BLOCKS, SIDE, SIDE * SIDE), ((0, 32),), -0.2, 0.2)), 0.25, 4.0),
        "source": draw_source(jax.random.fold_in(splits[3], 71), 0),
    }


RELAX_WEIGHT = 0.8
DIFFUSION_NUMBER = 1000.0

def blocks_to_grid(blocks):
    num_blocks, channels, edge_len = (blocks.shape[0], blocks.shape[1], blocks.shape[2])
    columns = num_blocks // 4
    parted = blocks.reshape(columns, 2, 2, channels, edge_len, edge_len, edge_len)
    parted = parted.transpose(3, 0, 6, 1, 4, 2, 5)
    return parted.reshape(channels, columns * edge_len, 4 * edge_len * edge_len)

def grid_to_blocks(grid):
    channels, length, plane = grid.shape
    edge_len = math.isqrt(plane) // 2
    columns = length // edge_len
    parted = grid.reshape(channels, columns, edge_len, 2, edge_len, 2, edge_len)
    parted = parted.transpose(1, 3, 5, 0, 4, 6, 2)
    return parted.reshape(columns * 4, channels, edge_len, edge_len * edge_len)

def flat_neighbors(array):
    plane = array.shape[2]
    width_y = math.isqrt(plane)
    middle = array[:, 1:-1]
    padded = jnp.pad(middle, ((0, 0), (0, 0), (width_y, width_y)))
    column = jnp.arange(plane) % width_y
    lower_y = jnp.where(column == 0, 0.0, padded[:, :, width_y - 1:width_y - 1 + plane])
    upper_y = jnp.where(column == width_y - 1, 0.0, padded[:, :, width_y + 1:width_y + 1 + plane])
    return (middle, (array[:, :-2], array[:, 2:], padded[:, :, 0:plane], padded[:, :, 2 * width_y:2 * width_y + plane], lower_y, upper_y))

def coefficients(viscous, level_coef, pad_along):
    middle, beside_all = flat_neighbors(pad_along(viscous))
    face_coef = tuple((0.5 * (middle + neighbor) for neighbor in beside_all))
    summed = face_coef[0] + face_coef[1] + face_coef[2] + face_coef[3] + face_coef[4] + face_coef[5]
    diagonal = 1.0 + level_coef * summed
    return (face_coef, diagonal)

def operate(solution, face_coef, diagonal, level_coef, pad_along):
    middle, beside_all = flat_neighbors(pad_along(solution))
    summed = face_coef[0] * beside_all[0]
    for index_no in range(1, 6):
        summed = summed + face_coef[index_no] * beside_all[index_no]
    return diagonal * solution - level_coef * summed

def smooth(solution, right_side, face_coef, diagonal, level_coef, pad_along, repeats):
    for sweep_no in range(repeats):
        solution = solution + RELAX_WEIGHT * (right_side - operate(solution, face_coef, diagonal, level_coef, pad_along)) / diagonal
    return solution

def coarsen(grid):
    channels, length, plane = grid.shape
    width_y = math.isqrt(plane)
    shaped = grid.reshape(channels, length // 2, 2, width_y // 2, 2, width_y // 2, 2)
    return shaped.mean(axis=(2, 4, 6)).reshape(channels, length // 2, plane // 4)

def refine(grid):
    channels, length, plane = grid.shape
    width_y = math.isqrt(plane)
    shaped = grid.reshape(channels, length, 1, width_y, 1, width_y, 1)
    shaped = jnp.broadcast_to(shaped, (channels, length, 2, width_y, 2, width_y, 2))
    return shaped.reshape(channels, 2 * length, 4 * plane)

def vcycle_solve(right_side, viscous, pad_along, bottom_solve):
    stored = []
    solution = right_side
    level_rhs = right_side
    for level_no in range(3):
        level_coef = DIFFUSION_NUMBER / 4.0 ** level_no
        face_coef, diagonal = coefficients(viscous, level_coef, pad_along)
        solution = smooth(solution, level_rhs, face_coef, diagonal, level_coef, pad_along, SWEEPS)
        residue = level_rhs - operate(solution, face_coef, diagonal, level_coef, pad_along)
        stored.append((solution, level_rhs, face_coef, diagonal, level_coef))
        level_rhs = coarsen(residue)
        viscous = coarsen(viscous)
        solution = jnp.zeros_like(level_rhs)
    solution = bottom_solve(level_rhs, viscous)
    for level_no in (2, 1, 0):
        before, level_rhs, face_coef, diagonal, level_coef = stored[level_no]
        solution = smooth(before + refine(solution), level_rhs, face_coef, diagonal, level_coef, pad_along, SWEEPS)
    return solution

def stream_pad(array):
    return jnp.pad(array, ((0, 0), (1, 1), (0, 0)))

def global_bottom(level_rhs, viscous):
    level_coef = DIFFUSION_NUMBER / 64.0
    face_coef, diagonal = coefficients(viscous, level_coef, stream_pad)
    return smooth(jnp.zeros_like(level_rhs), level_rhs, face_coef, diagonal, level_coef, stream_pad, BOTTOM)

def reference(velocity_old, viscosity_old, source):
    velocity = jnp.take(velocity_old, source, axis=0)
    viscous_new = jnp.take(viscosity_old, source, axis=0)
    right_side = blocks_to_grid(velocity)
    viscous = blocks_to_grid(viscous_new[:, None])
    solution = vcycle_solve(right_side, viscous, stream_pad, global_bottom)
    return grid_to_blocks(solution)
```

```python
import functools

import jax
import jax.numpy as jnp
from jax import lax
from jax.experimental import pallas as pl
from jax.experimental.pallas import tpu as pltpu
from jax.sharding import PartitionSpec as P


BOTTOM = 8
DIFFUSION_NUMBER = 1000.0
WEIGHT = 0.8
LANES = 128
MID = 8
F32 = jnp.float32
ANY = pl.BlockSpec(memory_space=pl.ANY)
WHOLE = pl.BlockSpec(memory_space=pltpu.VMEM)
SCALARS = pl.BlockSpec(memory_space=pltpu.SMEM)

HALO = 7
BASE0 = 8
BASE1 = 4
SIDE0 = 2
SIDE1 = 3
FETCHED = SIDE1 - 1
EDGES = 3 * FETCHED
REACH = 3
MEGA = 1024 * 1024


def iota(shape, axis):
    return lax.broadcasted_iota(jnp.int32, shape, axis)


def spin(value, shift, axis):
    size = value.shape[axis]
    return pltpu.roll(value, shift % size, axis)


def beside0(v):
    row = iota((MID, LANES), 0)
    low = spin(v[3 * MID :], 1, 0)
    low = jnp.where(row == 0, spin(low, 64, 1), low)
    high = spin(v[:MID], -1, 0)
    high = jnp.where(row == MID - 1, spin(high, 64, 1), high)
    return (
        jnp.concatenate([low, v[: 3 * MID]], axis=0),
        jnp.concatenate([v[MID:], high], axis=0),
        spin(v, 1, 1),
        spin(v, -1, 1),
    )


def beside1(v):
    row, lane = iota(v.shape, 0), iota(v.shape, 1)
    other = spin(v, 64, 1)
    down, up = spin(other, 1, 0), spin(other, -1, 0)
    down = jnp.where(row == 0, spin(down, 32, 1), down)
    up = jnp.where(row == MID - 1, spin(up, -32, 1), up)
    return (jnp.where(lane < 64, down, other), jnp.where(lane < 64, other, up), spin(v, 1, 1), spin(v, -1, 1))


def beside_packed(v, width):
    row = iota(v.shape, 0)
    down, up = spin(v, width, 0), spin(v, -width, 0)
    down = jnp.where(row < width, spin(down, 16, 1), down)
    up = jnp.where(row >= MID - width, spin(up, -16, 1), up)
    return (down, up, spin(v, width, 1), spin(v, -width, 1))


def beside2(v):
    return beside_packed(v, 1)


def beside3(v):
    return beside_packed(v, 2)


def outside(level):
    shape = (4 * MID if level == 0 else MID, LANES)
    row, lane = iota(shape, 0), iota(shape, 1)
    if level == 0:
        z = lane & 63
        return (row == 0) & (lane < 64), (row == 4 * MID - 1) & (lane >= 64), z == 0, z == 63
    if level == 1:
        z = lane & 31
        return (row == 0) & (lane < 32), (row == MID - 1) & (lane >= 96), z == 0, z == 31
    width = level - 1
    z, side = lane & 15, lane & 31
    return (row < width) & (side < 16), (row >= MID - width) & (side >= 16), z < width, z >= 16 - width


def over_layers(low, high, step, work):
    turns = (high - low) // step

    def body(t, _):
        for d in range(step):
            work(low + t * step + d)
        return 0

    if turns == 1:
        body(0, 0)
    else:
        lax.fori_loop(0, turns, body, 0)
    for i in range(low + turns * step, high):
        work(i)


def make_weights(level, beside, nu, coef, scale, back, low, high, first_x, total_x, step=2):
    level_coef = DIFFUSION_NUMBER / 4.0**level

    def work(i):
        mid = nu[i]
        out = outside(level)
        others = [nu[i - 1], nu[i + 1]] + [jnp.where(far, 0.0, v) for far, v in zip(out, beside(mid))]
        faces = [0.5 * (mid + other) for other in others]
        diag = 1.0 + level_coef * (faces[0] + faces[1] + faces[2] + faces[3] + faces[4] + faces[5])
        x = first_x + i
        weight = jnp.where((x >= 0) & (x < total_x), WEIGHT, 0.0)
        own = weight / diag
        scale[i] = own
        if back is not None:
            back[i] = diag * (1.0 / WEIGHT)
        own = own * level_coef
        for at, face in enumerate(faces):
            value = own * face
            coef[at, i] = value if at < 2 else jnp.where(out[at - 2], 0.0, value)

    over_layers(low, high, step, work)


def gathered_sum(beside, src, c, i, coef_i):
    mid = src[c, i]
    y_low, y_high, z_low, z_high = beside(mid)
    total = coef_i[0] * src[c, i - 1] + coef_i[1] * src[c, i + 1]
    total = total + (coef_i[2] * y_low + coef_i[3] * y_high)
    total = total + (coef_i[4] * z_low + coef_i[5] * z_high)
    return mid, total


def sweep(beside, src, dst, coef, right, comps, low, high, step=2, scale=None):
    def work(i):
        coef_i = [coef[at, i] for at in range(6)]
        for c in range(comps):
            mid, total = gathered_sum(beside, src, c, i, coef_i)
            if scale is not None:
                term = scale[i] * mid
                right[c, i] = term
            else:
                term = right[c, i]
            dst[c, i] = (total + term) + (1.0 - WEIGHT) * mid

    over_layers(low, high, step, work)


def residual(beside, src, coef, right, back, c, i, coef_i):
    mid, total = gathered_sum(beside, src, c, i, coef_i)
    return ((total + right[c, i]) - WEIGHT * mid) * back[i]


def from_zero(rhs, scale, right, dst, comps, low, high, step=2):
    def work(i):
        for c in range(comps):
            term = scale[i] * rhs[c, i]
            right[c, i] = term
            dst[c, i] = term

    over_layers(low, high, step, work)


def split_rows(lane):
    return lane // 64, (lane & 63) // 32, lane & 31


def matrix_0_1(factor, transposed=False):
    shape = (LANES, 2 * LANES) if transposed else (2 * LANES, LANES)
    fine, coarse = iota(shape, 1 if transposed else 0), iota(shape, 0 if transposed else 1)
    lane = fine & (LANES - 1)
    goal = (fine // LANES) * 64 + (lane // 64) * 32 + (lane & 63) // 2
    return jnp.where(goal == coarse, factor, 0.0).astype(jnp.bfloat16)


def matrix_1_2(field, factor, transposed=False):
    shape = (LANES, LANES)
    fine, coarse = iota(shape, 1 if transposed else 0), iota(shape, 0 if transposed else 1)
    goal = field * 32 + ((fine & 63) // 32) * 16 + (fine & 31) // 2
    return jnp.where(goal == coarse, factor, 0.0).astype(jnp.bfloat16)


def times(value, matrix):
    total = None
    for _ in range(3):
        part = value.astype(jnp.bfloat16)
        value = value - part.astype(F32)
        term = jnp.dot(part, matrix, preferred_element_type=F32)
        total = term if total is None else total + term
    return total


def pair_y(value):
    first = value[:MID] + value[MID : 2 * MID]
    second = value[2 * MID : 3 * MID] + value[3 * MID :]
    return first, second


def vmem(*shape):
    return pltpu.VMEM((*shape, LANES), F32)


def shaped(*dims):
    return jax.ShapeDtypeStruct((*dims, LANES), F32)


def start(copies):
    for copy in copies:
        copy.start()
    return copies


def finish(copies):
    for copy in copies:
        copy.wait()


def place_in_mesh():
    group, member = lax.axis_index("grp"), lax.axis_index("dev")
    return group, member, group * lax.axis_size("dev") + member


def slot_for(source, base, blocks, dst, owner):
    slot = 0
    for j in range(blocks):
        slot = jnp.where(lax.div(source[base + dst * blocks + j] - base, blocks) == owner, j, slot)
    return slot


def pick(viscosity, velocity, block, fields):
    parts, at = [], 0
    if fields[0] is None:
        parts.append((pl.ds(0, 1), viscosity.at[pl.ds(block, 1)]))
        fields, at = fields[1:], 1
    if fields:
        parts.append((pl.ds(at, len(fields)), velocity.at[block, pl.ds(fields[0], len(fields))]))
    return parts


def load_kernel(*refs):
    count = (len(refs) - 1) // 2
    copies = [
        pltpu.make_async_copy(array, out, refs[-1].at[n]) for n, (array, out) in enumerate(zip(refs[:count], refs[count:-1]))
    ]
    finish(start(copies))


def load(*arrays):
    arrays = [pltpu.with_memory_space_constraint(array, pltpu.HBM) for array in arrays]
    return pl.pallas_call(
        load_kernel,
        in_specs=[ANY] * len(arrays),
        out_specs=[WHOLE] * len(arrays),
        out_shape=[jax.ShapeDtypeStruct(array.shape, array.dtype) for array in arrays],
        scratch_shapes=[pltpu.SemaphoreType.DMA((len(arrays),))],
        compiler_params=pltpu.CompilerParams(vmem_limit_bytes=16 * MEGA),
        name="load",
    )(*arrays)


def pack_kernel(members, fields, sends, source, *refs):
    raw, outs = refs[: -len(sends)], refs[-len(sends) :]
    blocks = raw[0].shape[0]
    group, member, _ = place_in_mesh()
    base = group * members * blocks
    for out, (turn, owners) in zip(outs, sends):
        for at, n in enumerate(owners):
            slot = slot_for(source, base, blocks, member ^ turn, member ^ n)
            for f, field in enumerate(fields):
                out[at, f] = raw[2 * n][slot] if field is None else raw[2 * n + 1][slot, field]


def pack(source, raw, fields, members, sends):
    edge, flat = raw[0].shape[-2:]
    return pl.pallas_call(
        functools.partial(pack_kernel, members, fields, sends),
        in_specs=[SCALARS] + [WHOLE] * len(raw),
        out_specs=[WHOLE] * len(sends),
        out_shape=[jax.ShapeDtypeStruct((len(owners), len(fields), edge, flat), F32) for _, owners in sends],
        compiler_params=pltpu.CompilerParams(vmem_limit_bytes=16 * MEGA),
        name="pack",
    )(source, *raw)


def assemble_kernel(members, fields, sends, source, viscosity, velocity, viscosity_other, velocity_other, *refs):
    received, (own, facing, outer, tall, turned, sems) = refs[: len(sends)], refs[len(sends) :]
    blocks = viscosity.shape[0]
    edge = own.shape[1]
    group, member, _ = place_in_mesh()
    base = group * members * blocks

    def each_copy(act):
        for j in range(blocks):
            owner = lax.div(source[base + member * blocks + j] - base, blocks)
            rows = pl.ds((j % 2) * 64 + (j // 2) * edge, edge)
            for n, arrays in enumerate(((viscosity, velocity), (viscosity_other, velocity_other))):

                @pl.when(owner == member ^ n)
                def _(arrays=arrays):
                    for f, (goal, part) in enumerate(pick(*arrays, j, fields)):
                        act(pltpu.make_async_copy(part, tall.at[goal, rows], sems.at[j, f]))

            for part, (turn, owners) in zip(received, sends):
                for at, n in enumerate(owners):

                    @pl.when(owner == member ^ turn ^ n)
                    def _(part=part, at=at):
                        act(pltpu.make_async_copy(part.at[at], tall.at[:, rows], sems.at[j, 0]))

    each_copy(lambda copy: copy.start())
    each_copy(lambda copy: copy.wait())
    for f in range(len(fields)):
        for at in range(edge * edge // LANES):
            turned[f, pl.ds(at * LANES, LANES)] = tall[f, :, pl.ds(at * LANES, LANES)].T
        for i in range(edge):
            for lo in range(4):
                rows = pl.ds(lo * MID, MID)
                own[f, i, rows] = turned[f, pl.ds(lo * edge + i, MID, 4 * edge)]
    odd = (member & 1) == 1
    for goal, low in ((facing, jnp.where(odd, 0, edge - HALO)), (outer, jnp.where(odd, edge - HALO, 0))):
        for f in range(len(fields)):
            for i in range(HALO):
                goal[f, i] = own[f, low + i]


def assemble(source, raw, fields, received, members, sends):
    _, width, edge, flat = received[0].shape
    rows = flat // edge
    return pl.pallas_call(
        functools.partial(assemble_kernel, members, fields, sends),
        in_specs=[SCALARS] + [WHOLE] * (4 + len(sends)),
        out_specs=[WHOLE] * 3,
        scratch_shapes=[
            pltpu.VMEM((width, LANES, flat), F32),
            vmem(width, flat),
            pltpu.SemaphoreType.DMA((raw[0].shape[0], 2)),
        ],
        out_shape=[shaped(width, layers, rows) for layers in (edge, HALO, HALO)],
        compiler_params=pltpu.CompilerParams(vmem_limit_bytes=16 * MEGA),
        name="assemble",
    )(source, *raw, *received)


def copy_layers(target, first, source, at, count):
    def work(i):
        target[first + i] = source[at, i]

    over_layers(0, count, 4 if count % 4 == 0 else count, work)


def copy_halos(target, near, beyond, at, width, me):
    odd = (me & 1) == 1
    low, high = BASE0 - HALO, BASE0 + width
    copy_layers(target, jnp.where(odd, low, high), near, at, HALO)
    copy_layers(target, jnp.where(odd, high, low), beyond, at, HALO)


def viscosity_kernel(total_x, own, near, beyond, coef, scale, back, coef1, scale1, back1, nu2, nu, nu1, sums):
    width = own.shape[1]
    layers, layers1 = width + 2 * BASE0, width // 2 + 2 * BASE1
    _, _, me = place_in_mesh()
    copy_layers(nu, BASE0, own, 0, width)
    copy_halos(nu, near, beyond, 0, width, me)
    make_weights(0, beside0, nu, coef, scale, back, 2, layers - 2, me * width - BASE0, total_x, step=8)

    def nu_sums(t):
        a, b = pair_y(nu[2 + 2 * t] + nu[3 + 2 * t])
        sums[t, :, pl.ds(0, LANES)] = a
        sums[t, :, pl.ds(LANES, LANES)] = b

    count = layers1 - 2
    over_layers(0, count, count // 2, nu_sums)
    value = times(sums[...].reshape(count * MID, 2 * LANES), matrix_0_1(0.125))
    nu1[pl.ds(1, count)] = value.reshape(count, MID, LANES)
    make_weights(
        1, beside1, nu1, coef1, scale1, back1, 2, layers1 - 2, me * (width // 2) - BASE1, total_x // 2, step=8
    )
    mine = width // 4
    paired = [nu1[BASE1 + 2 * t] + nu1[BASE1 + 2 * t + 1] for t in range(mine)]
    value = times(jnp.concatenate(paired, axis=0), matrix_1_2(3, 0.125))
    nu2[...] = value.reshape(mine, MID, LANES)


def viscosity_weights(arrays, total_x):
    width, rows = arrays[0].shape[1:3]
    layers, layers1 = width + 2 * BASE0, width // 2 + 2 * BASE1
    return pl.pallas_call(
        functools.partial(viscosity_kernel, total_x),
        in_specs=[WHOLE] * 3,
        out_specs=[WHOLE] * 7,
        out_shape=[
            shaped(6, layers, rows), shaped(layers, rows), shaped(layers, rows),
            shaped(6, layers1, MID), shaped(layers1, MID), shaped(layers1, MID),
            shaped(width // 4, MID),
        ],
        scratch_shapes=[
            vmem(layers, rows), vmem(layers1, MID), pltpu.VMEM((layers1 - 2, MID, 2 * LANES), F32),
        ],
        compiler_params=pltpu.CompilerParams(vmem_limit_bytes=24 * MEGA),
        cost_estimate=pl.CostEstimate(flops=200_000_000, bytes_accessed=8_000_000, transcendentals=0),
        name="viscosity",
    )(*arrays)


def down_kernel(
    comp_at, first_field, own, near, beyond, coef, scale, back, coef1, scale1, back1, *refs,
):
    before, (A, right, B1, right1, message, B, sums, rhs1, A1) = refs[0], refs[1:]
    comps = len(comp_at)
    width = own.shape[1]
    layers, layers1 = width + 2 * BASE0, width // 2 + 2 * BASE1
    _, _, me = place_in_mesh()
    for c, at in enumerate(comp_at):
        copy_layers(A.at[c], BASE0, own, at, width)
        copy_halos(A.at[c], near, beyond, at, width, me)
    sweep(beside0, A, B, coef, right, comps, 2, layers - 2, scale=scale, step=11)
    sweep(beside0, B, A, coef, right, comps, 3, layers - 3, step=14)
    count = layers1 - 4

    def residual_sums(t):
        found = [None] * comps
        for d in range(2):
            i = 4 + 2 * t + d
            coef_i = [coef[at, i] for at in range(6)]
            for c in range(comps):
                value = residual(beside0, A, coef, right, back, c, i, coef_i)
                found[c] = value if d == 0 else found[c] + value
        for c in range(comps):
            a, b = pair_y(found[c])
            sums[c, t, :, pl.ds(0, LANES)] = a
            sums[c, t, :, pl.ds(LANES, LANES)] = b

    over_layers(0, count, 5, residual_sums)
    matrix = matrix_0_1(0.125)
    for c in range(comps):
        value = times(sums[c].reshape(count * MID, 2 * LANES), matrix)
        rhs1[c, pl.ds(2, count)] = value.reshape(count, MID, LANES)

    from_zero(rhs1, scale1, right1, A1, comps, 2, layers1 - 2, step=8)
    sweep(beside1, A1, B1, coef1, right1, comps, 3, layers1 - 3, step=11)
    mine = width // 4
    chained = before.shape[0] > mine
    total = before[pl.ds(EDGES if chained else 0, mine)].reshape(mine * MID, LANES)
    paired = [[] for _ in range(comps)]
    for t in range(mine):
        found = [None] * comps
        for d in range(2):
            i = BASE1 + 2 * t + d
            coef_i = [coef1[at, i] for at in range(6)]
            for c in range(comps):
                value = residual(beside1, B1, coef1, right1, back1, c, i, coef_i)
                found[c] = value if d == 0 else found[c] + value
        for c in range(comps):
            paired[c].append(found[c])
    for c in range(comps):
        total = total + times(jnp.concatenate(paired[c], axis=0), matrix_1_2(first_field + c, 0.125))
    message[pl.ds(EDGES, mine)] = total.reshape(mine, MID, LANES)

    first, last = BASE1 + 1, BASE1 + width // 2 - SIDE1
    odd = (me & 1) == 1
    for low, at in ((jnp.where(odd, first, last), 0), (jnp.where(odd, last, first), EDGES + mine)):
        if chained:
            message[pl.ds(at, EDGES)] = before[pl.ds(at, EDGES)]
        for c in range(comps):
            for t in range(FETCHED):
                message[at + (first_field + c) * FETCHED + t] = B1[c, low + t]


def down(arrays, comp_at, first_field, weights, before):
    width, rows = arrays[0].shape[1:3]
    comps = len(comp_at)
    layers, layers1, mine = width + 2 * BASE0, width // 2 + 2 * BASE1, width // 4
    return pl.pallas_call(
        functools.partial(down_kernel, comp_at, first_field),
        in_specs=[WHOLE] * 10,
        out_specs=[WHOLE] * 5,
        out_shape=[
            shaped(comps, layers, rows), shaped(comps, layers, rows),
            shaped(comps, layers1, MID), shaped(comps, layers1, MID),
            shaped(mine + 2 * EDGES, MID),
        ],
        scratch_shapes=[
            vmem(comps, layers, rows),
            pltpu.VMEM((comps, layers1 - 4, MID, 2 * LANES), F32),
            vmem(comps, layers1, MID), vmem(comps, layers1, MID),
        ],
        compiler_params=pltpu.CompilerParams(vmem_limit_bytes=24 * MEGA),
        cost_estimate=pl.CostEstimate(flops=200_000_000, bytes_accessed=8_000_000, transcendentals=0),
        name="down",
    )(*arrays, *weights, before)


def up_kernel(total_x, parts, *refs):
    (message, beside, beyond, far, other), refs = refs[:5], refs[5:]
    coef, coef1, refs = refs[0], refs[1], refs[2:]
    comps = []
    for part in parts:
        comps += [(*refs[:4], n) for n in range(part)]
        refs = refs[4:]
    out = refs[0]
    (
        A, B, refined, turned, blocks, A1, B1, refined1,
        window, A2, B2, nu2, coef2, scale2, back2, right2, A3, B3, nu3, coef3, scale3, right3, rhs3,
        out_sems,
    ) = refs[1:]
    width = blocks.shape[2]
    mine = width // 4
    _, _, me = place_in_mesh()

    layers2 = (2 * REACH + 1) * mine + 2
    own2 = 1 + REACH * mine
    first2 = me * mine - own2
    lane = iota((MID, LANES), 1)
    zeros = jnp.zeros((MID, LANES), F32)
    nu2[0] = zeros
    nu2[layers2 - 1] = zeros
    odd = (me & 1) == 1
    side = jnp.where(odd, -1, 1)
    theirs = mine + EDGES
    pieces = [(message, EDGES, 0), (beside, EDGES, side), (beyond, 0, -side), (beyond, theirs, -2 * side)]
    pieces += [(far, EDGES, -3 * side), (other, 0, 2 * side), (other, theirs, 3 * side)]
    for piece, at, place_of in pieces:
        goal = own2 + place_of * mine
        for i in range(mine):
            value = piece[at + i]
            window[goal + i] = value
            value = jnp.where(lane >= 96, value, 0.0)
            value = value + spin(value, 32, 1)
            nu2[goal + i] = value + spin(value, 64, 1)
    reach3 = 9
    low2, high2 = own2 - 2 * reach3 - 2, own2 + mine + 2 * reach3 + 2
    make_weights(2, beside2, nu2, coef2, scale2, back2, low2, high2, first2, total_x // 4, step=16)

    def zero2(i):
        term = scale2[i] * window[i]
        right2[0, i] = term
        A2[0, i] = term

    over_layers(low2, high2, 16, zero2)
    sweep(beside2, A2, B2, coef2, right2, 1, low2 + 1, high2 - 1, step=23)

    own3 = reach3 + 2
    mine3 = mine // 2
    row = iota((MID, LANES), 0)

    def both(value):
        value = value + jnp.where((row & 1) == 0, spin(value, -1, 0), spin(value, 1, 0))
        return (value + jnp.where((lane & 1) == 0, spin(value, -1, 1), spin(value, 1, 1))) * 0.125

    def nu_down(t):
        nu3[1 + t] = both(nu2[low2 + 2 * t] + nu2[low2 + 2 * t + 1])

    def rhs_down(t):
        total = None
        for d in range(2):
            i = low2 + 2 + 2 * t + d
            value = residual(beside2, B2, coef2, right2, back2, 0, i, [coef2[at, i] for at in range(6)])
            total = value if total is None else total + value
        rhs3[0, 2 + t] = both(total)

    over_layers(0, mine3 + 2 * reach3 + 2, 24, nu_down)
    over_layers(0, mine3 + 2 * reach3, 11, rhs_down)
    low3, high3 = own3 - reach3, own3 + mine3 + reach3
    make_weights(
        3, beside3, nu3, coef3, scale3, None, low3, high3, me * mine3 - own3, total_x // 8, step=high3 - low3
    )
    from_zero(rhs3, scale3, right3, A3, 1, low3, high3, step=high3 - low3)
    src, dst = A3, B3
    for turn in range(1, BOTTOM):
        low, high = low3 + turn, high3 - turn
        sweep(beside3, src, dst, coef3, right3, 1, low, high, step=high - low)
        src, dst = dst, src
    e3 = src

    for t in range(mine3 + 4):
        value = e3[0, own3 - 2 + t]
        for d in range(2):
            i = own2 - 4 + 2 * t + d
            A2[0, i] = B2[0, i] + value
    low, high = own2 - 3, own2 + mine + 3
    sweep(beside2, A2, B2, coef2, right2, 1, low, high, step=high - low)
    sweep(beside2, B2, A2, coef2, right2, 1, low + 1, high - 1, step=high - low - 2)

    count = mine + 4
    value = A2[0, pl.ds(own2 - 2, count)].reshape(count * MID, LANES)
    matrix = jnp.concatenate([matrix_1_2(c, 1.0, transposed=True) for c in range(3)], axis=1)
    refined1[...] = times(value, matrix).reshape(count, MID, 3 * LANES)
    low, high = BASE1 - SIDE1, BASE1 + width // 2 + SIDE1
    for t in range(count):
        for d in range(2):
            i = BASE1 - 4 + 2 * t + d
            if not low <= i < high:
                continue
            for c, (_, _, u1, _, n) in enumerate(comps):
                before, after = i - low, i - (high - FETCHED)
                if before < FETCHED or after >= 0:
                    edge = c * FETCHED + (before if before < FETCHED else after)
                    near, past = beside[edge], beyond[mine + edge]
                    value = jnp.where(odd, near, past) if before < FETCHED else jnp.where(odd, past, near)
                else:
                    value = u1[n, i]
                A1[c, i] = value + refined1[t, :, pl.ds(c * LANES, LANES)]
    rights1 = [(b1, n) for _, _, _, b1, n in comps]
    sweep_many(beside1, A1, B1, coef1, rights1, low + 1, high - 1, 0, 10)
    sweep_many(beside1, B1, A1, coef1, rights1, low + 2, high - 2, 0, 9)

    layers = width + 2 * SIDE0
    shift = BASE0 - SIDE0
    count = layers // 2
    matrix = matrix_0_1(1.0, transposed=True)
    for c in range(3):
        value = A1[c, pl.ds(BASE1 - SIDE0 // 2, count)].reshape(count * MID, LANES)
        refined[c] = times(value, matrix).reshape(count, MID, 2 * LANES)

    def add(t):
        for c, (u0, _, _, _, n) in enumerate(comps):
            a, b = refined[c, t, :, pl.ds(0, LANES)], refined[c, t, :, pl.ds(LANES, LANES)]
            value = jnp.concatenate([a, a, b, b], axis=0)
            for d in range(2):
                A[c, 2 * t + d] = u0[n, 2 * t + d + shift] + value

    over_layers(0, count, 6, add)
    rights = [(b0, n) for _, b0, _, _, n in comps]
    sweep_many(beside0, A, B, coef, rights, 1, layers - 1, shift, 8)
    sweep_many(beside0, B, A, coef, rights, SIDE0, layers - SIDE0, shift, 8)

    writes = []
    for c in range(3):
        for i in range(width):
            for lo in range(4):
                turned[c, pl.ds(lo * width + i, MID, 4 * width)] = A[c, SIDE0 + i, pl.ds(lo * MID, MID)]
        for at in range(width * width // LANES):
            tall = turned[c, pl.ds(at * LANES, LANES)].T
            for slot in range(4):
                first_row = (slot % 2) * 64 + (slot // 2) * width
                blocks[slot, c, :, pl.ds(at * LANES, LANES)] = tall[first_row : first_row + width]
        writes += start([pltpu.make_async_copy(blocks.at[:, c], out.at[:, c], out_sems.at[c])])
    finish(writes)


def sweep_many(beside, src, dst, coef, rights, low, high, shift, step):
    def work(i):
        coef_i = [coef[at, i + shift] for at in range(6)]
        for c, (right, n) in enumerate(rights):
            mid, total = gathered_sum(beside, src, c, i, coef_i)
            dst[c, i] = (total + right[n, i + shift]) + (1.0 - WEIGHT) * mid

    over_layers(low, high, step, work)


def up(pieces, weights, chunks, parts, width, total_x):
    rows = weights[0].shape[2]
    layers, layers1, mine = width + 2 * SIDE0, width // 2 + 2 * BASE1, width // 4
    layers2, layers3 = (2 * REACH + 1) * mine + 2, mine // 2 + 22
    out_shape = (4, 3, width, width * rows)
    operands = [*pieces, *weights]
    for chunk in chunks:
        operands += chunk
    return pl.pallas_call(
        functools.partial(up_kernel, total_x, parts),
        in_specs=[WHOLE] * len(operands),
        out_specs=ANY,
        out_shape=jax.ShapeDtypeStruct(out_shape, F32),
        scratch_shapes=[
            vmem(3, layers, rows), vmem(3, layers, rows),
            pltpu.VMEM((3, layers // 2, MID, 2 * LANES), F32), vmem(3, width * rows), pltpu.VMEM(out_shape, F32),
            vmem(3, layers1, MID), vmem(3, layers1, MID),
            pltpu.VMEM((mine + 4, MID, 3 * LANES), F32),
            vmem(layers2, MID), vmem(1, layers2, MID), vmem(1, layers2, MID), vmem(layers2, MID),
            vmem(6, layers2, MID), vmem(layers2, MID), vmem(layers2, MID), vmem(1, layers2, MID),
            vmem(1, layers3, MID), vmem(1, layers3, MID), vmem(layers3, MID),
            vmem(6, layers3, MID), vmem(layers3, MID), vmem(1, layers3, MID), vmem(1, layers3, MID),
            pltpu.SemaphoreType.DMA((3,)),
        ],
        compiler_params=pltpu.CompilerParams(vmem_limit_bytes=32 * MEGA),
        cost_estimate=pl.CostEstimate(flops=400_000_000, bytes_accessed=16_000_000, transcendentals=0),
        name="up",
    )(*operands)


def local(velocity_old, viscosity_old, source):
    axes = ("grp", "dev")
    members = lax.axis_size("dev")
    count = lax.axis_size("grp") * members
    edge = velocity_old.shape[2]
    total_x = count * edge
    turns = turn_order(members)
    pairs = [(m, m ^ 1) for m in range(members)]
    own_raw = load(viscosity_old, velocity_old)
    raw = (*own_raw, *(lax.ppermute(array, "dev", pairs) for array in (viscosity_old, velocity_old)))
    source = pltpu.with_memory_space_constraint(source, pltpu.HBM)

    chunks = ((None, 0), (1, 2))
    late = tuple((turn, (0, 1)) for turn in turns)
    early = ((turns[0], (0,)),)
    plans = (early + ((turns[0], (1,)),) + late[1:], late)
    received = []
    for fields, plan in zip(chunks, plans):
        packed = []
        if plan[0] in early:
            packed += pack(source, own_raw, fields, members, early)
        packed += pack(source, raw, fields, members, plan[len(packed) :])
        received.append(
            [lax.ppermute(sent, "dev", [(m, m ^ turn) for m in range(members)]) for (turn, _), sent in zip(plan, packed)]
        )

    def swap(array, hop):
        return lax.ppermute(array, axes, [(i, i ^ hop) for i in range(count)])

    def swap_outward(array, hop):
        goals = [(i, i + hop if i & hop else i - hop) for i in range(count)]
        return lax.ppermute(array, axes, [(i, to) for i, to in goals if 0 <= to < count])

    grids = []
    for fields, plan, slots in zip(chunks, plans, received):
        grid, facing, outer = assemble(source, raw, fields, slots, members, plan)
        beyond = swap_outward(outer, 1)
        grids.append((grid, swap(facing, 1), beyond))
    *weights, sent = viscosity_weights(grids[0], total_x)
    kept = []
    for fields, arrays in zip(chunks, grids):
        comps = [(at, field) for at, field in enumerate(fields) if field is not None]
        *state, sent = down(arrays, tuple(at for at, _ in comps), comps[0][1], weights, sent)
        kept.append(state)

    beside = swap(sent, 1)
    hops = [(i, i - 3 + 6 * (i % 2)) for i in range(count)]
    far = lax.ppermute(sent, axes, [(i, to) for i, to in hops if 0 <= to < count])
    mine = edge // 4
    beyond = swap_outward(jnp.concatenate([sent[EDGES:], beside[EDGES : EDGES + mine]], axis=0), 1)
    came, far = lax.optimization_barrier((beyond, far))
    other = swap(came, 1)
    widths = tuple(state[0].shape[0] for state in kept)
    return up((sent, beside, beyond, far, other), (weights[0], weights[3]), kept, widths, edge, total_x)


def turn_order(members):
    if members & (members - 1):
        raise ValueError("members")
    return tuple(range(members - 2, 0, -2))


def solution(mesh):
    return jax.shard_map(
        local,
        mesh=mesh,
        in_specs=(P(("grp", "dev"), None, None, None), P(("grp", "dev"), None, None), P()),
        out_specs=P(("grp", "dev"), None, None, None),
        check_vma=False,
    )
```

```python
import functools

import jax
import jax.numpy as jnp
from jax import lax
from jax.experimental import pallas as pl
from jax.experimental.pallas import tpu as pltpu
from jax.sharding import PartitionSpec as P


BOTTOM = 8
DIFFUSION_NUMBER = 1000.0
WEIGHT = 0.8
LANES = 128
MID = 8
F32 = jnp.float32
ANY = pl.BlockSpec(memory_space=pl.ANY)
WHOLE = pl.BlockSpec(memory_space=pltpu.VMEM)
SCALARS = pl.BlockSpec(memory_space=pltpu.SMEM)

HALO = 7
BASE0 = 8
BASE1 = 4
SIDE0 = 2
SIDE1 = 3
FETCHED = SIDE1 - 1
EDGES = 3 * FETCHED
REACH = 3
MEGA = 1024 * 1024


def iota(shape, axis):
    return lax.broadcasted_iota(jnp.int32, shape, axis)


def spin(value, shift, axis):
    size = value.shape[axis]
    return pltpu.roll(value, shift % size, axis)


def beside0(v):
    row = iota((MID, LANES), 0)
    low = spin(v[3 * MID :], 1, 0)
    low = jnp.where(row == 0, spin(low, 64, 1), low)
    high = spin(v[:MID], -1, 0)
    high = jnp.where(row == MID - 1, spin(high, 64, 1), high)
    return (
        jnp.concatenate([low, v[: 3 * MID]], axis=0),
        jnp.concatenate([v[MID:], high], axis=0),
        spin(v, 1, 1),
        spin(v, -1, 1),
    )


def beside1(v):
    row, lane = iota(v.shape, 0), iota(v.shape, 1)
    other = spin(v, 64, 1)
    down, up = spin(other, 1, 0), spin(other, -1, 0)
    down = jnp.where(row == 0, spin(down, 32, 1), down)
    up = jnp.where(row == MID - 1, spin(up, -32, 1), up)
    return (jnp.where(lane < 64, down, other), jnp.where(lane < 64, other, up), spin(v, 1, 1), spin(v, -1, 1))


def beside_packed(v, width):
    row = iota(v.shape, 0)
    down, up = spin(v, width, 0), spin(v, -width, 0)
    down = jnp.where(row < width, spin(down, 16, 1), down)
    up = jnp.where(row >= MID - width, spin(up, -16, 1), up)
    return (down, up, spin(v, width, 1), spin(v, -width, 1))


def beside2(v):
    return beside_packed(v, 1)


def beside3(v):
    return beside_packed(v, 2)


def outside(level):
    shape = (4 * MID if level == 0 else MID, LANES)
    row, lane = iota(shape, 0), iota(shape, 1)
    if level == 0:
        z = lane & 63
        return (row == 0) & (lane < 64), (row == 4 * MID - 1) & (lane >= 64), z == 0, z == 63
    if level == 1:
        z = lane & 31
        return (row == 0) & (lane < 32), (row == MID - 1) & (lane >= 96), z == 0, z == 31
    width = level - 1
    z, side = lane & 15, lane & 31
    return (row < width) & (side < 16), (row >= MID - width) & (side >= 16), z < width, z >= 16 - width


def over_layers(low, high, step, work):
    turns = (high - low) // step

    def body(t, _):
        for d in range(step):
            work(low + t * step + d)
        return 0

    if turns == 1:
        body(0, 0)
    else:
        lax.fori_loop(0, turns, body, 0)
    for i in range(low + turns * step, high):
        work(i)


def make_weights(level, beside, nu, coef, scale, back, low, high, first_x, total_x, step=2):
    level_coef = DIFFUSION_NUMBER / 4.0**level

    def work(i):
        mid = nu[i]
        out = outside(level)
        others = [nu[i - 1], nu[i + 1]] + [jnp.where(far, 0.0, v) for far, v in zip(out, beside(mid))]
        faces = [0.5 * (mid + other) for other in others]
        diag = 1.0 + level_coef * (faces[0] + faces[1] + faces[2] + faces[3] + faces[4] + faces[5])
        x = first_x + i
        weight = jnp.where((x >= 0) & (x < total_x), WEIGHT, 0.0)
        own = weight / diag
        scale[i] = own
        if back is not None:
            back[i] = diag * (1.0 / WEIGHT)
        own = own * level_coef
        for at, face in enumerate(faces):
            value = own * face
            coef[at, i] = value if at < 2 else jnp.where(out[at - 2], 0.0, value)

    over_layers(low, high, step, work)


def gathered_sum(beside, src, c, i, coef_i):
    mid = src[c, i]
    y_low, y_high, z_low, z_high = beside(mid)
    total = coef_i[0] * src[c, i - 1] + coef_i[1] * src[c, i + 1]
    total = total + (coef_i[2] * y_low + coef_i[3] * y_high)
    total = total + (coef_i[4] * z_low + coef_i[5] * z_high)
    return mid, total


def sweep(beside, src, dst, coef, right, comps, low, high, step=2, scale=None):
    def work(i):
        coef_i = [coef[at, i] for at in range(6)]
        for c in range(comps):
            mid, total = gathered_sum(beside, src, c, i, coef_i)
            if scale is not None:
                term = scale[i] * mid
                right[c, i] = term
            else:
                term = right[c, i]
            dst[c, i] = (total + term) + (1.0 - WEIGHT) * mid

    over_layers(low, high, step, work)


def residual(beside, src, coef, right, back, c, i, coef_i):
    mid, total = gathered_sum(beside, src, c, i, coef_i)
    return ((total + right[c, i]) - WEIGHT * mid) * back[i]


def from_zero(rhs, scale, right, dst, comps, low, high, step=2):
    def work(i):
        for c in range(comps):
            term = scale[i] * rhs[c, i]
            right[c, i] = term
            dst[c, i] = term

    over_layers(low, high, step, work)


def split_rows(lane):
    return lane // 64, (lane & 63) // 32, lane & 31


def matrix_0_1(factor, transposed=False):
    shape = (LANES, 2 * LANES) if transposed else (2 * LANES, LANES)
    fine, coarse = iota(shape, 1 if transposed else 0), iota(shape, 0 if transposed else 1)
    lane = fine & (LANES - 1)
    goal = (fine // LANES) * 64 + (lane // 64) * 32 + (lane & 63) // 2
    return jnp.where(goal == coarse, factor, 0.0).astype(jnp.bfloat16)


def matrix_1_2(field, factor, transposed=False):
    shape = (LANES, LANES)
    fine, coarse = iota(shape, 1 if transposed else 0), iota(shape, 0 if transposed else 1)
    goal = field * 32 + ((fine & 63) // 32) * 16 + (fine & 31) // 2
    return jnp.where(goal == coarse, factor, 0.0).astype(jnp.bfloat16)


def times(value, matrix):
    total = None
    for _ in range(3):
        part = value.astype(jnp.bfloat16)
        value = value - part.astype(F32)
        term = jnp.dot(part, matrix, preferred_element_type=F32)
        total = term if total is None else total + term
    return total


def pair_y(value):
    first = value[:MID] + value[MID : 2 * MID]
    second = value[2 * MID : 3 * MID] + value[3 * MID :]
    return first, second


def vmem(*shape):
    return pltpu.VMEM((*shape, LANES), F32)


def shaped(*dims):
    return jax.ShapeDtypeStruct((*dims, LANES), F32)


def start(copies):
    for copy in copies:
        copy.start()
    return copies


def finish(copies):
    for copy in copies:
        copy.wait()


def place_in_mesh():
    group, member = lax.axis_index("grp"), lax.axis_index("dev")
    return group, member, group * lax.axis_size("dev") + member


def slot_for(source, base, blocks, dst, owner):
    slot = 0
    for j in range(blocks):
        slot = jnp.where(lax.div(source[base + dst * blocks + j] - base, blocks) == owner, j, slot)
    return slot


def load_kernel(*refs):
    count = (len(refs) - 1) // 2
    copies = [
        pltpu.make_async_copy(array, out, refs[-1].at[n]) for n, (array, out) in enumerate(zip(refs[:count], refs[count:-1]))
    ]
    finish(start(copies))


def load(*arrays):
    arrays = [pltpu.with_memory_space_constraint(array, pltpu.HBM) for array in arrays]
    return pl.pallas_call(
        load_kernel,
        in_specs=[ANY] * len(arrays),
        out_specs=[WHOLE] * len(arrays),
        out_shape=[jax.ShapeDtypeStruct(array.shape, array.dtype) for array in arrays],
        scratch_shapes=[pltpu.SemaphoreType.DMA((len(arrays),))],
        compiler_params=pltpu.CompilerParams(vmem_limit_bytes=16 * MEGA),
        name="load",
    )(*arrays)


def early_kernel(members, fields, turn, source, viscosity, velocity, out, sems):
    group, member, _ = place_in_mesh()
    blocks = viscosity.shape[0]
    slot = slot_for(source, group * members * blocks, blocks, member ^ turn, member)
    copies = []
    for f, field in enumerate(fields):
        own = viscosity.at[slot] if field is None else velocity.at[slot, field]
        copies.append(pltpu.make_async_copy(own, out.at[0, f], sems.at[f]))
    finish(start(copies))


def early_pack(source, viscosity, velocity, fields, members, turn):
    return pl.pallas_call(
        functools.partial(early_kernel, members, fields, turn),
        in_specs=[SCALARS, ANY, ANY],
        out_specs=WHOLE,
        out_shape=jax.ShapeDtypeStruct((1, len(fields), *viscosity.shape[-2:]), F32),
        scratch_shapes=[pltpu.SemaphoreType.DMA((len(fields),))],
        compiler_params=pltpu.CompilerParams(vmem_limit_bytes=8 * MEGA),
        name="early",
    )(source, viscosity, velocity)


def pack_kernel(members, fields, sends, source, *refs):
    raw, outs = refs[: -len(sends)], refs[-len(sends) :]
    blocks = raw[0].shape[0]
    group, member, _ = place_in_mesh()
    base = group * members * blocks
    for out, (turn, owners) in zip(outs, sends):
        for at, n in enumerate(owners):
            slot = slot_for(source, base, blocks, member ^ turn, member ^ n)
            for f, field in enumerate(fields):
                out[at, f] = raw[2 * n][slot] if field is None else raw[2 * n + 1][slot, field]


def pack(source, raw, fields, members, sends):
    edge, flat = raw[0].shape[-2:]
    return pl.pallas_call(
        functools.partial(pack_kernel, members, fields, sends),
        in_specs=[SCALARS] + [WHOLE] * len(raw),
        out_specs=[WHOLE] * len(sends),
        out_shape=[jax.ShapeDtypeStruct((len(owners), len(fields), edge, flat), F32) for _, owners in sends],
        compiler_params=pltpu.CompilerParams(vmem_limit_bytes=16 * MEGA),
        name="pack",
    )(source, *raw)


def assemble_kernel(members, fields, sends, source, viscosity, velocity, viscosity_other, velocity_other, *refs):
    received, (own, facing, outer, tall, turned) = refs[: len(sends)], refs[len(sends) :]
    blocks = viscosity.shape[0]
    edge = own.shape[1]
    group, member, _ = place_in_mesh()
    base = group * members * blocks

    def gather(rows, values):
        for f, field in enumerate(fields):
            tall[f, rows] = values(f, field)

    for j in range(blocks):
        owner = lax.div(source[base + member * blocks + j] - base, blocks)
        rows = pl.ds((j % 2) * 64 + (j // 2) * edge, edge)
        for n, (visc, vel) in enumerate(((viscosity, velocity), (viscosity_other, velocity_other))):

            @pl.when(owner == member ^ n)
            def _(visc=visc, vel=vel):
                gather(rows, lambda f, field: visc[j] if field is None else vel[j, field])

        for part, (turn, owners) in zip(received, sends):
            for at, n in enumerate(owners):

                @pl.when(owner == member ^ turn ^ n)
                def _(part=part, at=at):
                    gather(rows, lambda f, field: part[at, f])

    for f in range(len(fields)):
        for at in range(edge * edge // LANES):
            turned[f, pl.ds(at * LANES, LANES)] = tall[f, :, pl.ds(at * LANES, LANES)].T
        for i in range(edge):
            for lo in range(4):
                rows = pl.ds(lo * MID, MID)
                own[f, i, rows] = turned[f, pl.ds(lo * edge + i, MID, 4 * edge)]
    odd = (member & 1) == 1
    for goal, low in ((facing, jnp.where(odd, 0, edge - HALO)), (outer, jnp.where(odd, edge - HALO, 0))):
        for f in range(len(fields)):
            for i in range(HALO):
                goal[f, i] = own[f, low + i]


def assemble(source, raw, fields, received, members, sends):
    _, width, edge, flat = received[0].shape
    rows = flat // edge
    return pl.pallas_call(
        functools.partial(assemble_kernel, members, fields, sends),
        in_specs=[SCALARS] + [WHOLE] * (4 + len(sends)),
        out_specs=[WHOLE] * 3,
        scratch_shapes=[
            pltpu.VMEM((width, LANES, flat), F32),
            vmem(width, flat),
        ],
        out_shape=[shaped(width, layers, rows) for layers in (edge, HALO, HALO)],
        compiler_params=pltpu.CompilerParams(vmem_limit_bytes=16 * MEGA),
        name="assemble",
    )(source, *raw, *received)


def copy_layers(target, first, source, at, count):
    def work(i):
        target[first + i] = source[at, i]

    over_layers(0, count, 4 if count % 4 == 0 else count, work)


def copy_halos(target, near, beyond, at, width, me):
    odd = (me & 1) == 1
    low, high = BASE0 - HALO, BASE0 + width
    copy_layers(target, jnp.where(odd, low, high), near, at, HALO)
    copy_layers(target, jnp.where(odd, high, low), beyond, at, HALO)


def viscosity_kernel(total_x, own, beyond, near, coef, scale, back, coef1, scale1, back1, nu2, nu, nu1, sums):
    width = own.shape[1]
    layers, layers1 = width + 2 * BASE0, width // 2 + 2 * BASE1
    _, _, me = place_in_mesh()
    copy_layers(nu, BASE0, own, 0, width)
    copy_halos(nu, near, beyond, 0, width, me)
    make_weights(0, beside0, nu, coef, scale, back, 2, layers - 2, me * width - BASE0, total_x, step=8)

    def nu_sums(t):
        a, b = pair_y(nu[2 + 2 * t] + nu[3 + 2 * t])
        sums[t, :, pl.ds(0, LANES)] = a
        sums[t, :, pl.ds(LANES, LANES)] = b

    count = layers1 - 2
    over_layers(0, count, count // 2, nu_sums)
    value = times(sums[...].reshape(count * MID, 2 * LANES), matrix_0_1(0.125))
    nu1[pl.ds(1, count)] = value.reshape(count, MID, LANES)
    make_weights(
        1, beside1, nu1, coef1, scale1, back1, 2, layers1 - 2, me * (width // 2) - BASE1, total_x // 2, step=8
    )
    mine = width // 4
    paired = [nu1[BASE1 + 2 * t] + nu1[BASE1 + 2 * t + 1] for t in range(mine)]
    value = times(jnp.concatenate(paired, axis=0), matrix_1_2(3, 0.125))
    nu2[...] = value.reshape(mine, MID, LANES)


def viscosity_weights(arrays, total_x):
    width, rows = arrays[0].shape[1:3]
    layers, layers1 = width + 2 * BASE0, width // 2 + 2 * BASE1
    return pl.pallas_call(
        functools.partial(viscosity_kernel, total_x),
        in_specs=[WHOLE] * 3,
        out_specs=[WHOLE] * 7,
        out_shape=[
            shaped(6, layers, rows), shaped(layers, rows), shaped(layers, rows),
            shaped(6, layers1, MID), shaped(layers1, MID), shaped(layers1, MID),
            shaped(width // 4, MID),
        ],
        scratch_shapes=[
            vmem(layers, rows), vmem(layers1, MID), pltpu.VMEM((layers1 - 2, MID, 2 * LANES), F32),
        ],
        compiler_params=pltpu.CompilerParams(vmem_limit_bytes=24 * MEGA),
        cost_estimate=pl.CostEstimate(flops=200_000_000, bytes_accessed=8_000_000, transcendentals=0),
        name="viscosity",
    )(*arrays)


def down_kernel(
    comp_at, first_field, own, beyond, near, coef, scale, back, coef1, scale1, back1, *refs,
):
    before, (A, right, B1, right1, message, B, sums, rhs1, A1) = refs[0], refs[1:]
    comps = len(comp_at)
    width = own.shape[1]
    layers, layers1 = width + 2 * BASE0, width // 2 + 2 * BASE1
    _, _, me = place_in_mesh()
    for c, at in enumerate(comp_at):
        copy_layers(A.at[c], BASE0, own, at, width)
        copy_halos(A.at[c], near, beyond, at, width, me)
    sweep(beside0, A, B, coef, right, comps, 2, layers - 2, scale=scale, step=11)
    sweep(beside0, B, A, coef, right, comps, 3, layers - 3, step=14)
    count = layers1 - 4

    def residual_sums(t):
        found = [None] * comps
        for d in range(2):
            i = 4 + 2 * t + d
            coef_i = [coef[at, i] for at in range(6)]
            for c in range(comps):
                value = residual(beside0, A, coef, right, back, c, i, coef_i)
                found[c] = value if d == 0 else found[c] + value
        for c in range(comps):
            a, b = pair_y(found[c])
            sums[c, t, :, pl.ds(0, LANES)] = a
            sums[c, t, :, pl.ds(LANES, LANES)] = b

    over_layers(0, count, 5, residual_sums)
    matrix = matrix_0_1(0.125)
    for c in range(comps):
        value = times(sums[c].reshape(count * MID, 2 * LANES), matrix)
        rhs1[c, pl.ds(2, count)] = value.reshape(count, MID, LANES)

    from_zero(rhs1, scale1, right1, A1, comps, 2, layers1 - 2, step=8)
    sweep(beside1, A1, B1, coef1, right1, comps, 3, layers1 - 3, step=11)
    mine = width // 4
    chained = before.shape[0] > mine
    total = before[pl.ds(EDGES if chained else 0, mine)].reshape(mine * MID, LANES)
    paired = [[] for _ in range(comps)]
    for t in range(mine):
        found = [None] * comps
        for d in range(2):
            i = BASE1 + 2 * t + d
            coef_i = [coef1[at, i] for at in range(6)]
            for c in range(comps):
                value = residual(beside1, B1, coef1, right1, back1, c, i, coef_i)
                found[c] = value if d == 0 else found[c] + value
        for c in range(comps):
            paired[c].append(found[c])
    for c in range(comps):
        total = total + times(jnp.concatenate(paired[c], axis=0), matrix_1_2(first_field + c, 0.125))
    message[pl.ds(EDGES, mine)] = total.reshape(mine, MID, LANES)

    first, last = BASE1 + 1, BASE1 + width // 2 - SIDE1
    odd = (me & 1) == 1
    for low, at in ((jnp.where(odd, first, last), 0), (jnp.where(odd, last, first), EDGES + mine)):
        if chained:
            message[pl.ds(at, EDGES)] = before[pl.ds(at, EDGES)]
        for c in range(comps):
            for t in range(FETCHED):
                message[at + (first_field + c) * FETCHED + t] = B1[c, low + t]


def down(arrays, comp_at, first_field, weights, before):
    width, rows = arrays[0].shape[1:3]
    comps = len(comp_at)
    layers, layers1, mine = width + 2 * BASE0, width // 2 + 2 * BASE1, width // 4
    return pl.pallas_call(
        functools.partial(down_kernel, comp_at, first_field),
        in_specs=[WHOLE] * 10,
        out_specs=[WHOLE] * 5,
        out_shape=[
            shaped(comps, layers, rows), shaped(comps, layers, rows),
            shaped(comps, layers1, MID), shaped(comps, layers1, MID),
            shaped(mine + 2 * EDGES, MID),
        ],
        scratch_shapes=[
            vmem(comps, layers, rows),
            pltpu.VMEM((comps, layers1 - 4, MID, 2 * LANES), F32),
            vmem(comps, layers1, MID), vmem(comps, layers1, MID),
        ],
        compiler_params=pltpu.CompilerParams(vmem_limit_bytes=24 * MEGA),
        cost_estimate=pl.CostEstimate(flops=200_000_000, bytes_accessed=8_000_000, transcendentals=0),
        name="down",
    )(*arrays, *weights, before)


def up_kernel(total_x, parts, *refs):
    (far, beyond, message, beside, other), refs = refs[:5], refs[5:]
    coef, coef1, refs = refs[0], refs[1], refs[2:]
    comps = []
    for part in parts:
        comps += [(*refs[:4], n) for n in range(part)]
        refs = refs[4:]
    out = refs[0]
    (
        A, B, refined, turned, blocks, A1, B1, refined1,
        window, A2, B2, nu2, coef2, scale2, back2, right2, A3, B3, nu3, coef3, scale3, right3, rhs3,
        out_sems,
    ) = refs[1:]
    width = blocks.shape[2]
    mine = width // 4
    _, _, me = place_in_mesh()

    layers2 = (2 * REACH + 1) * mine + 2
    own2 = 1 + REACH * mine
    first2 = me * mine - own2
    lane = iota((MID, LANES), 1)
    zeros = jnp.zeros((MID, LANES), F32)
    nu2[0] = zeros
    nu2[layers2 - 1] = zeros
    odd = (me & 1) == 1
    side = jnp.where(odd, -1, 1)
    theirs = mine + EDGES
    pieces = [(message, EDGES, 0), (beside, EDGES, side), (beyond, 0, -side), (beyond, theirs, -2 * side)]
    pieces += [(far, EDGES, -3 * side), (other, 0, 2 * side), (other, theirs, 3 * side)]
    for piece, at, place_of in pieces:
        goal = own2 + place_of * mine
        for i in range(mine):
            value = piece[at + i]
            window[goal + i] = value
            value = jnp.where(lane >= 96, value, 0.0)
            value = value + spin(value, 32, 1)
            nu2[goal + i] = value + spin(value, 64, 1)
    reach3 = 9
    low2, high2 = own2 - 2 * reach3 - 2, own2 + mine + 2 * reach3 + 2
    make_weights(2, beside2, nu2, coef2, scale2, back2, low2, high2, first2, total_x // 4, step=16)

    def zero2(i):
        term = scale2[i] * window[i]
        right2[0, i] = term
        A2[0, i] = term

    over_layers(low2, high2, 16, zero2)
    sweep(beside2, A2, B2, coef2, right2, 1, low2 + 1, high2 - 1, step=23)

    own3 = reach3 + 2
    mine3 = mine // 2
    row = iota((MID, LANES), 0)

    def both(value):
        value = value + jnp.where((row & 1) == 0, spin(value, -1, 0), spin(value, 1, 0))
        return (value + jnp.where((lane & 1) == 0, spin(value, -1, 1), spin(value, 1, 1))) * 0.125

    def nu_down(t):
        nu3[1 + t] = both(nu2[low2 + 2 * t] + nu2[low2 + 2 * t + 1])

    def rhs_down(t):
        total = None
        for d in range(2):
            i = low2 + 2 + 2 * t + d
            value = residual(beside2, B2, coef2, right2, back2, 0, i, [coef2[at, i] for at in range(6)])
            total = value if total is None else total + value
        rhs3[0, 2 + t] = both(total)

    over_layers(0, mine3 + 2 * reach3 + 2, 24, nu_down)
    over_layers(0, mine3 + 2 * reach3, 11, rhs_down)
    low3, high3 = own3 - reach3, own3 + mine3 + reach3
    make_weights(
        3, beside3, nu3, coef3, scale3, None, low3, high3, me * mine3 - own3, total_x // 8, step=high3 - low3
    )
    from_zero(rhs3, scale3, right3, A3, 1, low3, high3, step=high3 - low3)
    src, dst = A3, B3
    for turn in range(1, BOTTOM):
        low, high = low3 + turn, high3 - turn
        sweep(beside3, src, dst, coef3, right3, 1, low, high, step=high - low)
        src, dst = dst, src
    e3 = src

    for t in range(mine3 + 4):
        value = e3[0, own3 - 2 + t]
        for d in range(2):
            i = own2 - 4 + 2 * t + d
            A2[0, i] = B2[0, i] + value
    low, high = own2 - 3, own2 + mine + 3
    sweep(beside2, A2, B2, coef2, right2, 1, low, high, step=high - low)
    sweep(beside2, B2, A2, coef2, right2, 1, low + 1, high - 1, step=high - low - 2)

    count = mine + 4
    value = A2[0, pl.ds(own2 - 2, count)].reshape(count * MID, LANES)
    matrix = jnp.concatenate([matrix_1_2(c, 1.0, transposed=True) for c in range(3)], axis=1)
    refined1[...] = times(value, matrix).reshape(count, MID, 3 * LANES)
    low, high = BASE1 - SIDE1, BASE1 + width // 2 + SIDE1
    for t in range(count):
        for d in range(2):
            i = BASE1 - 4 + 2 * t + d
            if not low <= i < high:
                continue
            for c, (_, _, u1, _, n) in enumerate(comps):
                before, after = i - low, i - (high - FETCHED)
                if before < FETCHED or after >= 0:
                    edge = c * FETCHED + (before if before < FETCHED else after)
                    near, past = beside[edge], beyond[mine + edge]
                    value = jnp.where(odd, near, past) if before < FETCHED else jnp.where(odd, past, near)
                else:
                    value = u1[n, i]
                A1[c, i] = value + refined1[t, :, pl.ds(c * LANES, LANES)]
    rights1 = [(b1, n) for _, _, _, b1, n in comps]
    sweep_many(beside1, A1, B1, coef1, rights1, low + 1, high - 1, 0, 10)
    sweep_many(beside1, B1, A1, coef1, rights1, low + 2, high - 2, 0, 9)

    layers = width + 2 * SIDE0
    shift = BASE0 - SIDE0
    count = layers // 2
    matrix = matrix_0_1(1.0, transposed=True)
    for c in range(3):
        value = A1[c, pl.ds(BASE1 - SIDE0 // 2, count)].reshape(count * MID, LANES)
        refined[c] = times(value, matrix).reshape(count, MID, 2 * LANES)

    def add(t):
        for c, (u0, _, _, _, n) in enumerate(comps):
            a, b = refined[c, t, :, pl.ds(0, LANES)], refined[c, t, :, pl.ds(LANES, LANES)]
            value = jnp.concatenate([a, a, b, b], axis=0)
            for d in range(2):
                A[c, 2 * t + d] = u0[n, 2 * t + d + shift] + value

    over_layers(0, count, 6, add)
    rights = [(b0, n) for _, b0, _, _, n in comps]
    sweep_many(beside0, A, B, coef, rights, 1, layers - 1, shift, 8)
    sweep_many(beside0, B, A, coef, rights, SIDE0, layers - SIDE0, shift, 8)

    writes = []
    for c in range(3):
        for i in range(width):
            for lo in range(4):
                turned[c, pl.ds(lo * width + i, MID, 4 * width)] = A[c, SIDE0 + i, pl.ds(lo * MID, MID)]
        for at in range(width * width // LANES):
            tall = turned[c, pl.ds(at * LANES, LANES)].T
            for slot in range(4):
                first_row = (slot % 2) * 64 + (slot // 2) * width
                blocks[slot, c, :, pl.ds(at * LANES, LANES)] = tall[first_row : first_row + width]
        writes += start([pltpu.make_async_copy(blocks.at[:, c], out.at[:, c], out_sems.at[c])])
    finish(writes)


def sweep_many(beside, src, dst, coef, rights, low, high, shift, step):
    def work(i):
        coef_i = [coef[at, i + shift] for at in range(6)]
        for c, (right, n) in enumerate(rights):
            mid, total = gathered_sum(beside, src, c, i, coef_i)
            dst[c, i] = (total + right[n, i + shift]) + (1.0 - WEIGHT) * mid

    over_layers(low, high, step, work)


def up(pieces, weights, chunks, parts, width, total_x):
    rows = weights[0].shape[2]
    layers, layers1, mine = width + 2 * SIDE0, width // 2 + 2 * BASE1, width // 4
    layers2, layers3 = (2 * REACH + 1) * mine + 2, mine // 2 + 22
    out_shape = (4, 3, width, width * rows)
    operands = [*pieces, *weights]
    for chunk in chunks:
        operands += chunk
    return pl.pallas_call(
        functools.partial(up_kernel, total_x, parts),
        in_specs=[WHOLE] * len(operands),
        out_specs=ANY,
        out_shape=jax.ShapeDtypeStruct(out_shape, F32),
        scratch_shapes=[
            vmem(3, layers, rows), vmem(3, layers, rows),
            pltpu.VMEM((3, layers // 2, MID, 2 * LANES), F32), vmem(3, width * rows), pltpu.VMEM(out_shape, F32),
            vmem(3, layers1, MID), vmem(3, layers1, MID),
            pltpu.VMEM((mine + 4, MID, 3 * LANES), F32),
            vmem(layers2, MID), vmem(1, layers2, MID), vmem(1, layers2, MID), vmem(layers2, MID),
            vmem(6, layers2, MID), vmem(layers2, MID), vmem(layers2, MID), vmem(1, layers2, MID),
            vmem(1, layers3, MID), vmem(1, layers3, MID), vmem(layers3, MID),
            vmem(6, layers3, MID), vmem(layers3, MID), vmem(1, layers3, MID), vmem(1, layers3, MID),
            pltpu.SemaphoreType.DMA((3,)),
        ],
        compiler_params=pltpu.CompilerParams(vmem_limit_bytes=32 * MEGA),
        cost_estimate=pl.CostEstimate(flops=400_000_000, bytes_accessed=16_000_000, transcendentals=0),
        name="up",
    )(*operands)


def local(velocity_old, viscosity_old, source):
    axes = ("grp", "dev")
    members = lax.axis_size("dev")
    count = lax.axis_size("grp") * members
    edge = velocity_old.shape[2]
    total_x = count * edge
    turns = turn_order(members)
    pairs = [(m, m ^ 1) for m in range(members)]
    in_hbm = [pltpu.with_memory_space_constraint(array, pltpu.HBM) for array in (viscosity_old, velocity_old)]
    raw = (*load(viscosity_old, velocity_old), *(lax.ppermute(array, "dev", pairs) for array in (viscosity_old, velocity_old)))
    source = pltpu.with_memory_space_constraint(source, pltpu.HBM)

    chunks = ((None, 0), (1, 2))
    late = tuple((turn, (0, 1)) for turn in turns)
    early = ((turns[0], (0,)),)
    plans = (early + ((turns[0], (1,)),) + late[1:], late)
    received = []
    for fields, plan in zip(chunks, plans):
        packed = []
        if plan[0] in early:
            packed.append(early_pack(source, *in_hbm, fields, members, turns[0]))
        packed += pack(source, raw, fields, members, plan[len(packed) :])
        received.append(
            [lax.ppermute(sent, "dev", [(m, m ^ turn) for m in range(members)]) for (turn, _), sent in zip(plan, packed)]
        )

    def swap(array, hop):
        return lax.ppermute(array, axes, [(i, i ^ hop) for i in range(count)])

    def swap_outward(array, hop):
        goals = [(i, i + hop if i & hop else i - hop) for i in range(count)]
        return lax.ppermute(array, axes, [(i, to) for i, to in goals if 0 <= to < count])

    grids = []
    for fields, plan, slots in zip(chunks, plans, received):
        grid, facing, outer = assemble(source, raw, fields, slots, members, plan)
        beyond = swap_outward(outer, 1)
        grids.append((grid, beyond, swap(facing, 1)))
    *weights, sent = viscosity_weights(grids[0], total_x)
    kept = []
    for fields, arrays in zip(chunks, grids):
        comps = [(at, field) for at, field in enumerate(fields) if field is not None]
        *state, sent = down(arrays, tuple(at for at, _ in comps), comps[0][1], weights, sent)
        kept.append(state)

    beside = swap(sent, 1)
    hops = [(i, i - 3 + 6 * (i % 2)) for i in range(count)]
    far = lax.ppermute(sent, axes, [(i, to) for i, to in hops if 0 <= to < count])
    mine = edge // 4
    beyond = swap_outward(jnp.concatenate([sent[EDGES:], beside[EDGES : EDGES + mine]], axis=0), 1)
    came, far = lax.optimization_barrier((beyond, far))
    other = swap(came, 1)
    widths = tuple(state[0].shape[0] for state in kept)
    return up((far, beyond, sent, beside, other), (weights[0], weights[3]), kept, widths, edge, total_x)


def turn_order(members):
    if members & (members - 1):
        raise ValueError("members")
    return tuple(range(members - 2, 0, -2))


def solution(mesh):
    return jax.shard_map(
        local,
        mesh=mesh,
        in_specs=(P(("grp", "dev"), None, None, None), P(("grp", "dev"), None, None), P()),
        out_specs=P(("grp", "dev"), None, None, None),
        check_vma=False,
    )
```

```python
import functools

import jax
import jax.numpy as jnp
from jax import lax
from jax.experimental import pallas as pl
from jax.experimental.pallas import tpu as pltpu
from jax.sharding import PartitionSpec as P


BOTTOM = 8
DIFFUSION_NUMBER = 1000.0
WEIGHT = 0.8
LANES = 128
MID = 8
F32 = jnp.float32
ANY = pl.BlockSpec(memory_space=pl.ANY)
WHOLE = pl.BlockSpec(memory_space=pltpu.VMEM)
SCALARS = pl.BlockSpec(memory_space=pltpu.SMEM)

HALO = 7
BASE0 = 8
BASE1 = 4
SIDE0 = 2
SIDE1 = 3
FETCHED = SIDE1 - 1
EDGES = 3 * FETCHED
SPARE = 4
REACH = 3
MEGA = 1024 * 1024


def iota(shape, axis):
    return lax.broadcasted_iota(jnp.int32, shape, axis)


def spin(value, shift, axis):
    size = value.shape[axis]
    return pltpu.roll(value, shift % size, axis)


def beside0(v):
    row = iota((MID, LANES), 0)
    low = spin(v[3 * MID :], 1, 0)
    low = jnp.where(row == 0, spin(low, 64, 1), low)
    high = spin(v[:MID], -1, 0)
    high = jnp.where(row == MID - 1, spin(high, 64, 1), high)
    return (
        jnp.concatenate([low, v[: 3 * MID]], axis=0),
        jnp.concatenate([v[MID:], high], axis=0),
        spin(v, 1, 1),
        spin(v, -1, 1),
    )


def beside1(v):
    row, lane = iota(v.shape, 0), iota(v.shape, 1)
    other = spin(v, 64, 1)
    down, up = spin(other, 1, 0), spin(other, -1, 0)
    down = jnp.where(row == 0, spin(down, 32, 1), down)
    up = jnp.where(row == MID - 1, spin(up, -32, 1), up)
    return (jnp.where(lane < 64, down, other), jnp.where(lane < 64, other, up), spin(v, 1, 1), spin(v, -1, 1))


def beside_packed(v, width):
    row = iota(v.shape, 0)
    down, up = spin(v, width, 0), spin(v, -width, 0)
    down = jnp.where(row < width, spin(down, 16, 1), down)
    up = jnp.where(row >= MID - width, spin(up, -16, 1), up)
    return (down, up, spin(v, width, 1), spin(v, -width, 1))


def beside2(v):
    return beside_packed(v, 1)


def beside3(v):
    return beside_packed(v, 2)


def outside(level):
    shape = (4 * MID if level == 0 else MID, LANES)
    row, lane = iota(shape, 0), iota(shape, 1)
    if level == 0:
        z = lane & 63
        return (row == 0) & (lane < 64), (row == 4 * MID - 1) & (lane >= 64), z == 0, z == 63
    if level == 1:
        z = lane & 31
        return (row == 0) & (lane < 32), (row == MID - 1) & (lane >= 96), z == 0, z == 31
    width = level - 1
    z, side = lane & 15, lane & 31
    return (row < width) & (side < 16), (row >= MID - width) & (side >= 16), z < width, z >= 16 - width


def over_layers(low, high, step, work):
    turns = (high - low) // step

    def body(t, _):
        for d in range(step):
            work(low + t * step + d)
        return 0

    if turns == 1:
        body(0, 0)
    else:
        lax.fori_loop(0, turns, body, 0)
    for i in range(low + turns * step, high):
        work(i)


def make_weights(level, beside, nu, coef, scale, back, low, high, first_x, total_x, step=2):
    level_coef = DIFFUSION_NUMBER / 4.0**level

    def work(i):
        mid = nu[i]
        out = outside(level)
        others = [nu[i - 1], nu[i + 1]] + [jnp.where(far, 0.0, v) for far, v in zip(out, beside(mid))]
        faces = [0.5 * (mid + other) for other in others]
        diag = 1.0 + level_coef * (faces[0] + faces[1] + faces[2] + faces[3] + faces[4] + faces[5])
        x = first_x + i
        weight = jnp.where((x >= 0) & (x < total_x), WEIGHT, 0.0)
        own = weight / diag
        scale[i] = own
        if back is not None:
            back[i] = diag * (1.0 / WEIGHT)
        own = own * level_coef
        for at, face in enumerate(faces):
            value = own * face
            coef[at, i] = value if at < 2 else jnp.where(out[at - 2], 0.0, value)

    over_layers(low, high, step, work)


def gathered_sum(beside, src, c, i, coef_i):
    mid = src[c, i]
    y_low, y_high, z_low, z_high = beside(mid)
    total = coef_i[0] * src[c, i - 1] + coef_i[1] * src[c, i + 1]
    total = total + (coef_i[2] * y_low + coef_i[3] * y_high)
    total = total + (coef_i[4] * z_low + coef_i[5] * z_high)
    return mid, total


def sweep(beside, src, dst, coef, right, comps, low, high, step=2, scale=None):
    def work(i):
        coef_i = [coef[at, i] for at in range(6)]
        for c in range(comps):
            mid, total = gathered_sum(beside, src, c, i, coef_i)
            if scale is not None:
                term = scale[i] * mid
                right[c, i] = term
            else:
                term = right[c, i]
            dst[c, i] = (total + term) + (1.0 - WEIGHT) * mid

    over_layers(low, high, step, work)


def residual(beside, src, coef, right, back, c, i, coef_i):
    mid, total = gathered_sum(beside, src, c, i, coef_i)
    return ((total + right[c, i]) - WEIGHT * mid) * back[i]


def from_zero(rhs, scale, right, dst, comps, low, high, step=2):
    def work(i):
        for c in range(comps):
            term = scale[i] * rhs[c, i]
            right[c, i] = term
            dst[c, i] = term

    over_layers(low, high, step, work)


def split_rows(lane):
    return lane // 64, (lane & 63) // 32, lane & 31


def matrix_0_1(factor, transposed=False):
    shape = (LANES, 2 * LANES) if transposed else (2 * LANES, LANES)
    fine, coarse = iota(shape, 1 if transposed else 0), iota(shape, 0 if transposed else 1)
    lane = fine & (LANES - 1)
    goal = (fine // LANES) * 64 + (lane // 64) * 32 + (lane & 63) // 2
    return jnp.where(goal == coarse, factor, 0.0).astype(jnp.bfloat16)


def matrix_1_2(field, factor, transposed=False):
    shape = (LANES, LANES)
    fine, coarse = iota(shape, 1 if transposed else 0), iota(shape, 0 if transposed else 1)
    goal = field * 32 + ((fine & 63) // 32) * 16 + (fine & 31) // 2
    return jnp.where(goal == coarse, factor, 0.0).astype(jnp.bfloat16)


def times(value, matrix):
    total = None
    for _ in range(3):
        part = value.astype(jnp.bfloat16)
        value = value - part.astype(F32)
        term = jnp.dot(part, matrix, preferred_element_type=F32)
        total = term if total is None else total + term
    return total


def pair_y(value):
    first = value[:MID] + value[MID : 2 * MID]
    second = value[2 * MID : 3 * MID] + value[3 * MID :]
    return first, second


def vmem(*shape):
    return pltpu.VMEM((*shape, LANES), F32)


def shaped(*dims):
    return jax.ShapeDtypeStruct((*dims, LANES), F32)


def start(copies):
    for copy in copies:
        copy.start()
    return copies


def finish(copies):
    for copy in copies:
        copy.wait()


def place_in_mesh():
    group, member = lax.axis_index("grp"), lax.axis_index("dev")
    return group, member, group * lax.axis_size("dev") + member


def slot_for(source, base, blocks, dst, owner):
    slot = 0
    for j in range(blocks):
        slot = jnp.where(lax.div(source[base + dst * blocks + j] - base, blocks) == owner, j, slot)
    return slot


def load_kernel(*refs):
    count = (len(refs) - 1) // 2
    copies = [
        pltpu.make_async_copy(array, out, refs[-1].at[n]) for n, (array, out) in enumerate(zip(refs[:count], refs[count:-1]))
    ]
    finish(start(copies))


def load(*arrays):
    arrays = [pltpu.with_memory_space_constraint(array, pltpu.HBM) for array in arrays]
    return pl.pallas_call(
        load_kernel,
        in_specs=[ANY] * len(arrays),
        out_specs=[WHOLE] * len(arrays),
        out_shape=[jax.ShapeDtypeStruct(array.shape, array.dtype) for array in arrays],
        scratch_shapes=[pltpu.SemaphoreType.DMA((len(arrays),))],
        compiler_params=pltpu.CompilerParams(vmem_limit_bytes=16 * MEGA),
        name="load",
    )(*arrays)


def early_kernel(members, fields, turn, source, viscosity, velocity, out, sems):
    group, member, _ = place_in_mesh()
    blocks = viscosity.shape[0]
    slot = slot_for(source, group * members * blocks, blocks, member ^ turn, member)
    copies = []
    for f, field in enumerate(fields):
        own = viscosity.at[slot] if field is None else velocity.at[slot, field]
        copies.append(pltpu.make_async_copy(own, out.at[0, f], sems.at[f]))
    finish(start(copies))


def early_pack(source, viscosity, velocity, fields, members, turn):
    return pl.pallas_call(
        functools.partial(early_kernel, members, fields, turn),
        in_specs=[SCALARS, ANY, ANY],
        out_specs=WHOLE,
        out_shape=jax.ShapeDtypeStruct((1, len(fields), *viscosity.shape[-2:]), F32),
        scratch_shapes=[pltpu.SemaphoreType.DMA((len(fields),))],
        compiler_params=pltpu.CompilerParams(vmem_limit_bytes=8 * MEGA),
        name="early",
    )(source, viscosity, velocity)


def pack_kernel(members, fields, sends, source, *refs):
    raw, outs = refs[: -len(sends)], refs[-len(sends) :]
    blocks = raw[0].shape[0]
    group, member, _ = place_in_mesh()
    base = group * members * blocks
    for out, (turn, owners) in zip(outs, sends):
        for at, n in enumerate(owners):
            slot = slot_for(source, base, blocks, member ^ turn, member ^ n)
            for f, field in enumerate(fields):
                out[at, f] = raw[2 * n][slot] if field is None else raw[2 * n + 1][slot, field]


def pack(source, raw, fields, members, sends):
    edge, flat = raw[0].shape[-2:]
    return pl.pallas_call(
        functools.partial(pack_kernel, members, fields, sends),
        in_specs=[SCALARS] + [WHOLE] * len(raw),
        out_specs=[WHOLE] * len(sends),
        out_shape=[jax.ShapeDtypeStruct((len(owners), len(fields), edge, flat), F32) for _, owners in sends],
        compiler_params=pltpu.CompilerParams(vmem_limit_bytes=16 * MEGA),
        name="pack",
    )(source, *raw)


def assemble_kernel(members, fields, sends, source, viscosity, velocity, viscosity_other, velocity_other, *refs):
    received, (own, facing, outer, tall, turned) = refs[: len(sends)], refs[len(sends) :]
    blocks = viscosity.shape[0]
    edge = own.shape[1]
    group, member, _ = place_in_mesh()
    base = group * members * blocks

    def gather(rows, values):
        for f, field in enumerate(fields):
            tall[f, rows] = values(f, field)

    for j in range(blocks):
        owner = lax.div(source[base + member * blocks + j] - base, blocks)
        rows = pl.ds((j % 2) * 64 + (j // 2) * edge, edge)
        for n, (visc, vel) in enumerate(((viscosity, velocity), (viscosity_other, velocity_other))):

            @pl.when(owner == member ^ n)
            def _(visc=visc, vel=vel):
                gather(rows, lambda f, field: visc[j] if field is None else vel[j, field])

        for part, (turn, owners) in zip(received, sends):
            for at, n in enumerate(owners):

                @pl.when(owner == member ^ turn ^ n)
                def _(part=part, at=at):
                    gather(rows, lambda f, field: part[at, f])

    for f in range(len(fields)):
        for at in range(edge * edge // LANES):
            turned[f, pl.ds(at * LANES, LANES)] = tall[f, :, pl.ds(at * LANES, LANES)].T
        for i in range(edge):
            for lo in range(4):
                rows = pl.ds(lo * MID, MID)
                own[f, i, rows] = turned[f, pl.ds(lo * edge + i, MID, 4 * edge)]
    odd = (member & 1) == 1
    for goal, low in ((facing, jnp.where(odd, 0, edge - HALO)), (outer, jnp.where(odd, edge - HALO, 0))):
        for f in range(len(fields)):
            for i in range(HALO):
                goal[f, i] = own[f, low + i]


def assemble(source, raw, fields, received, members, sends):
    _, width, edge, flat = received[0].shape
    rows = flat // edge
    return pl.pallas_call(
        functools.partial(assemble_kernel, members, fields, sends),
        in_specs=[SCALARS] + [WHOLE] * (4 + len(sends)),
        out_specs=[WHOLE] * 3,
        scratch_shapes=[
            pltpu.VMEM((width, LANES, flat), F32),
            vmem(width, flat),
        ],
        out_shape=[shaped(width, layers, rows) for layers in (edge, HALO, HALO)],
        compiler_params=pltpu.CompilerParams(vmem_limit_bytes=16 * MEGA),
        name="assemble",
    )(source, *raw, *received)


def copy_layers(target, first, source, at, count):
    def work(i):
        target[first + i] = source[at, i]

    over_layers(0, count, 4 if count % 4 == 0 else count, work)


def copy_halos(target, near, beyond, at, width, me):
    odd = (me & 1) == 1
    low, high = BASE0 - HALO, BASE0 + width
    copy_layers(target, jnp.where(odd, low, high), near, at, HALO)
    copy_layers(target, jnp.where(odd, high, low), beyond, at, HALO)


def viscosity_kernel(total_x, own, beyond, near, coef, scale, back, coef1, scale1, back1, nu2, nu, nu1, sums):
    width = own.shape[1]
    layers, layers1 = width + 2 * BASE0, width // 2 + 2 * BASE1
    _, _, me = place_in_mesh()
    copy_layers(nu, BASE0, own, 0, width)
    copy_halos(nu, near, beyond, 0, width, me)
    make_weights(0, beside0, nu, coef, scale, back, 2, layers - 2, me * width - BASE0, total_x, step=11)

    def nu_sums(t):
        a, b = pair_y(nu[2 + 2 * t] + nu[3 + 2 * t])
        sums[t, :, pl.ds(0, LANES)] = a
        sums[t, :, pl.ds(LANES, LANES)] = b

    count = layers1 - 2
    over_layers(0, count, count // 2, nu_sums)
    value = times(sums[...].reshape(count * MID, 2 * LANES), matrix_0_1(0.125))
    nu1[pl.ds(1, count)] = value.reshape(count, MID, LANES)
    make_weights(
        1, beside1, nu1, coef1, scale1, back1, 2, layers1 - 2, me * (width // 2) - BASE1, total_x // 2, step=8
    )
    mine = width // 4
    paired = [nu1[BASE1 + 2 * t] + nu1[BASE1 + 2 * t + 1] for t in range(mine)]
    value = times(jnp.concatenate(paired, axis=0), matrix_1_2(3, 0.125))
    nu2[...] = value.reshape(mine, MID, LANES)


def viscosity_weights(arrays, total_x):
    width, rows = arrays[0].shape[1:3]
    layers, layers1 = width + 2 * BASE0, width // 2 + 2 * BASE1
    return pl.pallas_call(
        functools.partial(viscosity_kernel, total_x),
        in_specs=[WHOLE] * 3,
        out_specs=[WHOLE] * 7,
        out_shape=[
            shaped(6, layers, rows), shaped(layers, rows), shaped(layers, rows),
            shaped(6, layers1, MID), shaped(layers1, MID), shaped(layers1, MID),
            shaped(width // 4, MID),
        ],
        scratch_shapes=[
            vmem(layers, rows), vmem(layers1, MID), pltpu.VMEM((layers1 - 2, MID, 2 * LANES), F32),
        ],
        compiler_params=pltpu.CompilerParams(vmem_limit_bytes=24 * MEGA),
        cost_estimate=pl.CostEstimate(flops=200_000_000, bytes_accessed=8_000_000, transcendentals=0),
        name="viscosity",
    )(*arrays)


def down_kernel(
    comp_at, first_field, own, beyond, near, coef, scale, back, coef1, scale1, back1, *refs,
):
    before, (A, right, B1, right1, message, B, sums, rhs1, A1) = refs[0], refs[1:]
    comps = len(comp_at)
    width = own.shape[1]
    layers, layers1 = width + 2 * BASE0, width // 2 + 2 * BASE1
    _, _, me = place_in_mesh()
    for c, at in enumerate(comp_at):
        copy_layers(A.at[c], BASE0, own, at, width)
        copy_halos(A.at[c], near, beyond, at, width, me)
    sweep(beside0, A, B, coef, right, comps, 2, layers - 2, scale=scale, step=22)
    sweep(beside0, B, A, coef, right, comps, 3, layers - 3, step=21)
    count = layers1 - 4

    def residual_sums(t):
        found = [None] * comps
        for d in range(2):
            i = 4 + 2 * t + d
            coef_i = [coef[at, i] for at in range(6)]
            for c in range(comps):
                value = residual(beside0, A, coef, right, back, c, i, coef_i)
                found[c] = value if d == 0 else found[c] + value
        for c in range(comps):
            a, b = pair_y(found[c])
            sums[c, t, :, pl.ds(0, LANES)] = a
            sums[c, t, :, pl.ds(LANES, LANES)] = b

    over_layers(0, count, 10, residual_sums)
    matrix = matrix_0_1(0.125)
    for c in range(comps):
        value = times(sums[c].reshape(count * MID, 2 * LANES), matrix)
        rhs1[c, pl.ds(2, count)] = value.reshape(count, MID, LANES)

    from_zero(rhs1, scale1, right1, A1, comps, 2, layers1 - 2, step=8)
    sweep(beside1, A1, B1, coef1, right1, comps, 3, layers1 - 3, step=11)
    mine = width // 4
    chained = before.shape[0] > mine
    total = before[pl.ds(EDGES if chained else 0, mine)].reshape(mine * MID, LANES)
    paired = [[] for _ in range(comps)]
    for t in range(mine):
        found = [None] * comps
        for d in range(2):
            i = BASE1 + 2 * t + d
            coef_i = [coef1[at, i] for at in range(6)]
            for c in range(comps):
                value = residual(beside1, B1, coef1, right1, back1, c, i, coef_i)
                found[c] = value if d == 0 else found[c] + value
        for c in range(comps):
            paired[c].append(found[c])
    for c in range(comps):
        total = total + times(jnp.concatenate(paired[c], axis=0), matrix_1_2(first_field + c, 0.125))
    message[pl.ds(EDGES, mine)] = total.reshape(mine, MID, LANES)

    first, last = BASE1 + 1, BASE1 + width // 2 - SIDE1
    odd = (me & 1) == 1
    for low, at in ((jnp.where(odd, first, last), 0), (jnp.where(odd, last, first), EDGES + mine)):
        if chained:
            message[pl.ds(at, EDGES)] = before[pl.ds(at, EDGES)]
        for c in range(comps):
            for t in range(FETCHED):
                message[at + (first_field + c) * FETCHED + t] = B1[c, low + t]


def down(arrays, comp_at, first_field, weights, before):
    width, rows = arrays[0].shape[1:3]
    comps = len(comp_at)
    layers, layers1, mine = width + 2 * BASE0, width // 2 + 2 * BASE1, width // 4
    return pl.pallas_call(
        functools.partial(down_kernel, comp_at, first_field),
        in_specs=[WHOLE] * 10,
        out_specs=[WHOLE] * 5,
        out_shape=[
            shaped(comps, layers, rows), shaped(comps, layers, rows),
            shaped(comps, layers1, MID), shaped(comps, layers1, MID),
            shaped(mine + 2 * EDGES + SPARE, MID),
        ],
        scratch_shapes=[
            vmem(comps, layers, rows),
            pltpu.VMEM((comps, layers1 - 4, MID, 2 * LANES), F32),
            vmem(comps, layers1, MID), vmem(comps, layers1, MID),
        ],
        compiler_params=pltpu.CompilerParams(vmem_limit_bytes=24 * MEGA),
        cost_estimate=pl.CostEstimate(flops=200_000_000, bytes_accessed=8_000_000, transcendentals=0),
        name="down",
    )(*arrays, *weights, before)


def up_kernel(total_x, parts, *refs):
    (far, beyond, message, beside, other), refs = refs[:5], refs[5:]
    coef, coef1, refs = refs[0], refs[1], refs[2:]
    comps = []
    for part in parts:
        comps += [(*refs[:4], n) for n in range(part)]
        refs = refs[4:]
    out = refs[0]
    (
        A, B, refined, turned, blocks, A1, B1, refined1,
        window, A2, B2, nu2, coef2, scale2, back2, right2, A3, B3, nu3, coef3, scale3, right3, rhs3,
        out_sems,
    ) = refs[1:]
    width = blocks.shape[2]
    mine = width // 4
    _, _, me = place_in_mesh()

    layers2 = (2 * REACH + 1) * mine + 2
    own2 = 1 + REACH * mine
    first2 = me * mine - own2
    lane = iota((MID, LANES), 1)
    zeros = jnp.zeros((MID, LANES), F32)
    nu2[0] = zeros
    nu2[layers2 - 1] = zeros
    odd = (me & 1) == 1
    side = jnp.where(odd, -1, 1)
    theirs = mine + EDGES
    pieces = [(message, EDGES, 0), (beside, EDGES, side), (beyond, 0, -side), (beyond, theirs, -2 * side)]
    pieces += [(far, EDGES, -3 * side), (other, 0, 2 * side), (other, theirs, 3 * side)]
    for piece, at, place_of in pieces:
        goal = own2 + place_of * mine
        for i in range(mine):
            value = piece[at + i]
            window[goal + i] = value
            value = jnp.where(lane >= 96, value, 0.0)
            value = value + spin(value, 32, 1)
            nu2[goal + i] = value + spin(value, 64, 1)
    reach3 = 9
    low2, high2 = own2 - 2 * reach3 - 2, own2 + mine + 2 * reach3 + 2
    make_weights(2, beside2, nu2, coef2, scale2, back2, low2, high2, first2, total_x // 4, step=16)

    def zero2(i):
        term = scale2[i] * window[i]
        right2[0, i] = term
        A2[0, i] = term

    over_layers(low2, high2, 16, zero2)
    sweep(beside2, A2, B2, coef2, right2, 1, low2 + 1, high2 - 1, step=23)

    own3 = reach3 + 2
    mine3 = mine // 2
    row = iota((MID, LANES), 0)

    def both(value):
        value = value + jnp.where((row & 1) == 0, spin(value, -1, 0), spin(value, 1, 0))
        return (value + jnp.where((lane & 1) == 0, spin(value, -1, 1), spin(value, 1, 1))) * 0.125

    def nu_down(t):
        nu3[1 + t] = both(nu2[low2 + 2 * t] + nu2[low2 + 2 * t + 1])

    def rhs_down(t):
        total = None
        for d in range(2):
            i = low2 + 2 + 2 * t + d
            value = residual(beside2, B2, coef2, right2, back2, 0, i, [coef2[at, i] for at in range(6)])
            total = value if total is None else total + value
        rhs3[0, 2 + t] = both(total)

    over_layers(0, mine3 + 2 * reach3 + 2, 24, nu_down)
    over_layers(0, mine3 + 2 * reach3, 11, rhs_down)
    low3, high3 = own3 - reach3, own3 + mine3 + reach3
    make_weights(
        3, beside3, nu3, coef3, scale3, None, low3, high3, me * mine3 - own3, total_x // 8, step=high3 - low3
    )
    from_zero(rhs3, scale3, right3, A3, 1, low3, high3, step=high3 - low3)
    src, dst = A3, B3
    for turn in range(1, BOTTOM):
        low, high = low3 + turn, high3 - turn
        sweep(beside3, src, dst, coef3, right3, 1, low, high, step=high - low)
        src, dst = dst, src
    e3 = src

    for t in range(mine3 + 4):
        value = e3[0, own3 - 2 + t]
        for d in range(2):
            i = own2 - 4 + 2 * t + d
            A2[0, i] = B2[0, i] + value
    low, high = own2 - 3, own2 + mine + 3
    sweep(beside2, A2, B2, coef2, right2, 1, low, high, step=high - low)
    sweep(beside2, B2, A2, coef2, right2, 1, low + 1, high - 1, step=high - low - 2)

    count = mine + 4
    value = A2[0, pl.ds(own2 - 2, count)].reshape(count * MID, LANES)
    matrix = jnp.concatenate([matrix_1_2(c, 1.0, transposed=True) for c in range(3)], axis=1)
    refined1[...] = times(value, matrix).reshape(count, MID, 3 * LANES)
    low, high = BASE1 - SIDE1, BASE1 + width // 2 + SIDE1
    for t in range(count):
        for d in range(2):
            i = BASE1 - 4 + 2 * t + d
            if not low <= i < high:
                continue
            for c, (_, _, u1, _, n) in enumerate(comps):
                before, after = i - low, i - (high - FETCHED)
                if before < FETCHED or after >= 0:
                    edge = c * FETCHED + (before if before < FETCHED else after)
                    near, past = beside[edge], beyond[mine + edge]
                    value = jnp.where(odd, near, past) if before < FETCHED else jnp.where(odd, past, near)
                else:
                    value = u1[n, i]
                A1[c, i] = value + refined1[t, :, pl.ds(c * LANES, LANES)]
    rights1 = [(b1, n) for _, _, _, b1, n in comps]
    sweep_many(beside1, A1, B1, coef1, rights1, low + 1, high - 1, 0, 10)
    sweep_many(beside1, B1, A1, coef1, rights1, low + 2, high - 2, 0, 9)

    layers = width + 2 * SIDE0
    shift = BASE0 - SIDE0
    count = layers // 2
    matrix = matrix_0_1(1.0, transposed=True)
    for c in range(3):
        value = A1[c, pl.ds(BASE1 - SIDE0 // 2, count)].reshape(count * MID, LANES)
        refined[c] = times(value, matrix).reshape(count, MID, 2 * LANES)

    def add(t):
        for c, (u0, _, _, _, n) in enumerate(comps):
            a, b = refined[c, t, :, pl.ds(0, LANES)], refined[c, t, :, pl.ds(LANES, LANES)]
            value = jnp.concatenate([a, a, b, b], axis=0)
            for d in range(2):
                A[c, 2 * t + d] = u0[n, 2 * t + d + shift] + value

    over_layers(0, count, 6, add)
    rights = [(b0, n) for _, b0, _, _, n in comps]
    sweep_many(beside0, A, B, coef, rights, 1, layers - 1, shift, 17)
    sweep_many(beside0, B, A, coef, rights, SIDE0, layers - SIDE0, shift, 16)

    writes = []
    for c in range(3):
        for i in range(width):
            for lo in range(4):
                turned[c, pl.ds(lo * width + i, MID, 4 * width)] = A[c, SIDE0 + i, pl.ds(lo * MID, MID)]
        for at in range(width * width // LANES):
            tall = turned[c, pl.ds(at * LANES, LANES)].T
            for slot in range(4):
                first_row = (slot % 2) * 64 + (slot // 2) * width
                blocks[slot, c, :, pl.ds(at * LANES, LANES)] = tall[first_row : first_row + width]
        writes += start([pltpu.make_async_copy(blocks.at[:, c], out.at[:, c], out_sems.at[c])])
    finish(writes)


def sweep_many(beside, src, dst, coef, rights, low, high, shift, step):
    def work(i):
        coef_i = [coef[at, i + shift] for at in range(6)]
        for c, (right, n) in enumerate(rights):
            mid, total = gathered_sum(beside, src, c, i, coef_i)
            dst[c, i] = (total + right[n, i + shift]) + (1.0 - WEIGHT) * mid

    over_layers(low, high, step, work)


def up(pieces, weights, chunks, parts, width, total_x):
    rows = weights[0].shape[2]
    layers, layers1, mine = width + 2 * SIDE0, width // 2 + 2 * BASE1, width // 4
    layers2, layers3 = (2 * REACH + 1) * mine + 2, mine // 2 + 22
    out_shape = (4, 3, width, width * rows)
    operands = [*pieces, *weights]
    for chunk in chunks:
        operands += chunk
    return pl.pallas_call(
        functools.partial(up_kernel, total_x, parts),
        in_specs=[WHOLE] * len(operands),
        out_specs=ANY,
        out_shape=jax.ShapeDtypeStruct(out_shape, F32),
        scratch_shapes=[
            vmem(3, layers, rows), vmem(3, layers, rows),
            pltpu.VMEM((3, layers // 2, MID, 2 * LANES), F32), vmem(3, width * rows), pltpu.VMEM(out_shape, F32),
            vmem(3, layers1, MID), vmem(3, layers1, MID),
            pltpu.VMEM((mine + 4, MID, 3 * LANES), F32),
            vmem(layers2, MID), vmem(1, layers2, MID), vmem(1, layers2, MID), vmem(layers2, MID),
            vmem(6, layers2, MID), vmem(layers2, MID), vmem(layers2, MID), vmem(1, layers2, MID),
            vmem(1, layers3, MID), vmem(1, layers3, MID), vmem(layers3, MID),
            vmem(6, layers3, MID), vmem(layers3, MID), vmem(1, layers3, MID), vmem(1, layers3, MID),
            pltpu.SemaphoreType.DMA((3,)),
        ],
        compiler_params=pltpu.CompilerParams(vmem_limit_bytes=32 * MEGA),
        cost_estimate=pl.CostEstimate(flops=400_000_000, bytes_accessed=16_000_000, transcendentals=0),
        name="up",
    )(*operands)


def local(velocity_old, viscosity_old, source):
    axes = ("grp", "dev")
    members = lax.axis_size("dev")
    count = lax.axis_size("grp") * members
    edge = velocity_old.shape[2]
    total_x = count * edge
    turns = turn_order(members)
    pairs = [(m, m ^ 1) for m in range(members)]
    in_hbm = [pltpu.with_memory_space_constraint(array, pltpu.HBM) for array in (viscosity_old, velocity_old)]
    raw = (*load(viscosity_old, velocity_old), *(lax.ppermute(array, "dev", pairs) for array in (viscosity_old, velocity_old)))
    source = pltpu.with_memory_space_constraint(source, pltpu.HBM)

    chunks = ((None, 0), (1, 2))
    late = tuple((turn, (0, 1)) for turn in turns)
    early = ((turns[0], (0,)),)
    plans = (early + ((turns[0], (1,)),) + late[1:], late)
    received = []
    for fields, plan in zip(chunks, plans):
        packed = []
        if plan[0] in early:
            packed.append(early_pack(source, *in_hbm, fields, members, turns[0]))
        packed += pack(source, raw, fields, members, plan[len(packed) :])
        received.append(
            [lax.ppermute(sent, "dev", [(m, m ^ turn) for m in range(members)]) for (turn, _), sent in zip(plan, packed)]
        )

    def swap(array, hop):
        return lax.ppermute(array, axes, [(i, i ^ hop) for i in range(count)])

    def swap_outward(array, hop):
        goals = [(i, i + hop if i & hop else i - hop) for i in range(count)]
        return lax.ppermute(array, axes, [(i, to) for i, to in goals if 0 <= to < count])

    grids = []
    for fields, plan, slots in zip(chunks, plans, received):
        grid, facing, outer = assemble(source, raw, fields, slots, members, plan)
        beyond = swap_outward(outer, 1)
        grids.append((grid, beyond, swap(facing, 1)))
    *weights, sent = viscosity_weights(grids[0], total_x)
    kept = []
    for fields, arrays in zip(chunks, grids):
        comps = [(at, field) for at, field in enumerate(fields) if field is not None]
        *state, sent = down(arrays, tuple(at for at, _ in comps), comps[0][1], weights, sent)
        kept.append(state)

    beside = swap(sent, 1)
    hops = [(i, i - 3 + 6 * (i % 2)) for i in range(count)]
    far = lax.ppermute(sent, axes, [(i, to) for i, to in hops if 0 <= to < count])
    mine = edge // 4
    beyond = swap_outward(jnp.concatenate([sent[EDGES : mine + 2 * EDGES], beside[EDGES : EDGES + mine]], axis=0), 1)
    came, far = lax.optimization_barrier((beyond, far))
    other = swap(came, 1)
    widths = tuple(state[0].shape[0] for state in kept)
    return up((far, beyond, sent, beside, other), (weights[0], weights[3]), kept, widths, edge, total_x)


def turn_order(members):
    if members & (members - 1):
        raise ValueError("members")
    return tuple(range(members - 2, 0, -2))


def solution(mesh):
    return jax.shard_map(
        local,
        mesh=mesh,
        in_specs=(P(("grp", "dev"), None, None, None), P(("grp", "dev"), None, None), P()),
        out_specs=P(("grp", "dev"), None, None, None),
        check_vma=False,
    )
```
